512 devices in a mesh: grp: 16 (over y, core), se: 32 (over x, z).
Axes of the slice: x: 4, y: 8, z: 8, core: 2. Of those that a mesh axis runs over, the one named last changes fastest.
Arguments:
- pressure: bfloat16 [12288, 64, 128], P(('grp', 'se')), may hold values from -6 to 6
- block_owner: int32 [12288], P(('grp', 'se')), may hold values from 0 to 31, as said below
- level_one: bfloat16 [512, 256, 6144], P(('grp', 'se')), may hold values from -0.078125 to 0.078125
- level_one_map: int32 [512, 256], P(('grp', 'se')), may hold values from 0 to 4095, as said below
- level_two: bfloat16 [16, 128, 4096], P('grp', None, 'se'), may hold values from -0.375 to 0.375
- level_two_map: int32 [16, 16, 128], P('grp'), may hold values from 0 to 4095
Outputs:
- level_two_load: float32 [16, 64, 4096], P('grp', None, 'se')
- root_load: float32 [64, 4096], P(None, ('grp', 'se'))
The draws below stay inside these ranges and needn't reach their ends.
Inputs may be any that keep to these rules, and one draw needn't show every extreme that they name: `block_owner`: in each group (32 devices of 24 blocks each) one device holds at most 2 blocks for one superelement, and at most 48 blocks load one superelement; both bounds are reached in every group. `level_one_map`: for each first-level superelement, at most 16 of its boundary degrees of freedom map into one block j * 128 to (j + 1) * 128 - 1 of the group interior, and exactly 16 do for some block, for every superelement.
All inputs are finite; a program needn't handle non-finite values.
Results may differ from the reference program's by a relative error of at most 0.017.
Values may be sent and summed in bfloat16 or wider, within the bound.
No kernel may reach another device: no remote copies, remote signals or barrier semaphores. Data moves between devices by JAX's collectives and lax.ppermute only.
A program may use at most 64 MiB of HBM per device.

```python
import jax
import jax.numpy as jnp
from jax import lax

LC = 64
PANEL = 128
PB_DEV = 24
B1 = 256
I2H = 128
B2 = 128
ROOT = 4096
NGRP = 16
NSE = 32
NL2 = 16
SE1 = 512
BLOCKS = 12288
KMAX = 48
RC = 16
I1 = 6144
I2 = 256
G2 = 4096


def owner_group(key):
    key_pair, key_delta, key_order, key_shuffle = jax.random.split(key, 4)
    ordering = jax.random.permutation(key_pair, NSE)
    halfway = NSE // 2
    deltas = jax.random.randint(key_delta, (halfway,), 0, PB_DEV)
    deltas = deltas.at[0].set(PB_DEV)
    se_loads = jnp.zeros((NSE,), jnp.int32).at[ordering[:halfway]].set(PB_DEV + deltas)
    se_loads = se_loads.at[ordering[halfway:]].set(PB_DEV - deltas)
    dealing = jax.random.permutation(key_order, NSE)
    bounds = jnp.cumsum(se_loads[dealing])
    tokens = jnp.arange(PB_DEV, dtype=jnp.int32)[None, :] * NSE + jnp.arange(NSE, dtype=jnp.int32)[:, None]
    position = jnp.sum((bounds[None, None, :] <= tokens[:, :, None]).astype(jnp.int32), axis=2)
    owners = dealing[position]
    shuffles = jax.vmap(lambda single: jax.random.permutation(single, PB_DEV))(jax.random.split(key_shuffle, NSE))
    owners = jnp.take_along_axis(owners, shuffles, axis=1)
    return owners.reshape(-1).astype(jnp.int32)


def draw_block_owner(key, part):
    group_keys = jax.random.split(key, NGRP)
    return jax.vmap(owner_group)(group_keys).reshape(-1).astype(jnp.int32)


def one_map(key):
    key_fav, key_perm, key_offset = jax.random.split(key, 3)
    total = NSE * RC
    favourite = jax.random.randint(key_fav, (), 0, NSE).astype(jnp.int32)
    token_ids = jnp.arange(total, dtype=jnp.int32)
    scores = jax.random.permutation(key_perm, total).astype(jnp.int32)
    scores = jnp.where(token_ids // RC == favourite, token_ids % RC - total, scores)
    chosen = jnp.argsort(scores, stable=True)[:B1].astype(jnp.int32)
    owners = chosen // RC
    offsets = jax.random.randint(key_offset, (B1,), 0, I2H).astype(jnp.int32)
    return (owners * I2H + offsets).astype(jnp.int32)


def draw_level_one_map(key, part):
    keys = jax.random.split(key, SE1)
    return jax.vmap(one_map)(keys).astype(jnp.int32)


def plant(values, own_key, smallest, top_value):
    longest = values.shape.index(max(values.shape))
    spots = []
    for shift in (0, 1):
        where = [jax.random.randint(jax.random.fold_in(own_key, axis), (), 0, length) for axis, length in enumerate(values.shape)]
        where[longest] = (where[longest] + shift) % values.shape[longest]
        spots.append(tuple(where))
    return values.at[spots[0]].set(smallest).at[spots[1]].set(top_value)


def steps_of(key, shape, pieces, least, top_value):
    loudness = 1.0
    for dim, parts in pieces:
        draws = jax.random.uniform(jax.random.fold_in(jax.random.fold_in(key, 6), dim), (parts,), jnp.float32, least / len(pieces), top_value / len(pieces))
        loudness = loudness * jnp.repeat(jnp.exp(draws), shape[dim] // parts).reshape((-1,) + (1,) * (len(shape) - 1 - dim))
    return loudness


def bell_draw(own_key, extent, spread, most, cuts=(), held_as=jnp.bfloat16):
    result = spread * jax.random.normal(own_key, extent, jnp.float32)
    if cuts:
        result = result * steps_of(own_key, extent, cuts, -0.22, 0.18)
    return jnp.clip(result, -most, most).astype(held_as)


def setup_inputs(seed: int = 0) -> dict:
    seeds = jax.random.split(jax.random.key(seed), 7)
    return {
        "pressure": bell_draw(seeds[0], (BLOCKS, LC, PANEL), 1.0, 6.0, ((0, 512),)),
        "block_owner": draw_block_owner(jax.random.fold_in(seeds[6], 71), 0),
        "level_one": bell_draw(seeds[2], (SE1, B1, I1), I1 ** -0.5, 0.078125, ((0, 512),)),
        "level_one_map": draw_level_one_map(jax.random.fold_in(seeds[6], 71), 0),
        "level_two": bell_draw(seeds[4], (NGRP, B2, G2), I2 ** -0.5, 0.375, ((0, 16), (2, 32))),
        "level_two_map": plant(jax.random.randint(seeds[5], (NGRP, NL2, B2), 0, ROOT), jax.random.fold_in(seeds[5], 1), 0, ROOT - 1).astype(jnp.int32),
    }


def group_ranks(owner_rows):
    targets = jnp.arange(NSE, dtype=jnp.int32)
    hits = (owner_rows[:, None] == targets[None, :]).astype(jnp.int32)
    return jnp.sum(jnp.cumsum(hits, axis=0) * hits, axis=1) - 1


def condense_one(operands):
    interior, matrix = operands
    flat = interior.transpose(1, 0, 2).reshape(LC, KMAX * PANEL)
    return lax.dot_general(flat, matrix, (((1,), (1,)), ((), ())), preferred_element_type=jnp.float32)


def assemble(values, targets):
    return jnp.zeros((LC, G2), jnp.float32).at[:, targets].add(values)


def reference(pressure, block_owner, level_one, level_one_map, level_two, level_two_map):
    owner_rows = block_owner.reshape(NGRP, NSE * PB_DEV)
    ranks = jax.vmap(group_ranks)(owner_rows).reshape(-1).astype(jnp.int32)
    groups = (jnp.arange(BLOCKS, dtype=jnp.int32) // (NSE * PB_DEV)).astype(jnp.int32)
    element = groups * NSE + block_owner
    interior = jnp.zeros((SE1, KMAX, LC, PANEL), jnp.bfloat16).at[element, ranks].set(pressure)
    boundary = lax.map(condense_one, (interior, level_one))
    values = boundary.reshape(NGRP, NSE, LC, B1).transpose(0, 2, 1, 3).reshape(NGRP, LC, NSE * B1)
    targets = level_one_map.reshape(NGRP, NSE * B1)
    level_two_load = jax.vmap(assemble)(values, targets)
    loads = level_two_load.astype(jnp.bfloat16)
    left = loads.reshape(NGRP, LC, NL2, I2).astype(jnp.float32)
    right = level_two.reshape(NGRP, B2, NL2, I2).astype(jnp.float32)
    second = jnp.einsum("gcmi,gbmi->gmcb", left, right, precision=lax.Precision.HIGHEST)
    flat_second = second.transpose(2, 0, 1, 3).reshape(LC, NGRP * NL2 * B2)
    root_load = jnp.zeros((LC, ROOT), jnp.float32).at[:, level_two_map.reshape(-1)].add(flat_second)
    return level_two_load, root_load
```

```python
import jax
import jax.numpy as jnp
from jax import lax
from jax.experimental import pallas as pl
from jax.experimental.pallas import tpu as pltpu
from jax.sharding import PartitionSpec as P

ROOT = 4096
CAPACITY = 2
RC = 16
EMPTY = 64.0
BF16 = jnp.bfloat16
F32 = jnp.float32
I32 = jnp.int32
VMEM = pl.BlockSpec(memory_space=pltpu.VMEM)
SMEM = pl.BlockSpec(memory_space=pltpu.SMEM)
LIMIT = pltpu.CompilerParams(vmem_limit_bytes=24 * 1024 * 1024)


def iota(shape, dim):
    return lax.broadcasted_iota(I32, shape, dim)


def dot_nt(a, b):
    return lax.dot_general(a, b, (((1,), (1,)), ((), ())), preferred_element_type=F32)


def pack_kernel(owner_ref, pressure_ref, out_ref, count_ref):
    blocks = pressure_ref.shape[0]
    slots = out_ref.shape[0]
    members = slots // CAPACITY
    out_ref[:, 0:16, :] = jnp.full((slots, 16, out_ref.shape[2]), EMPTY, BF16)
    for e in range(members):
        count_ref[e] = 0
    for t in range(blocks):
        owner = owner_ref[t]
        count = count_ref[owner]
        count_ref[owner] = count + 1
        out_ref[owner * CAPACITY + count] = pressure_ref[t]


def pack(block_owner, pressure, members):
    _, cases, rows = pressure.shape
    return pl.pallas_call(
        pack_kernel,
        out_shape=jax.ShapeDtypeStruct((members * CAPACITY, cases, rows), BF16),
        in_specs=[SMEM, VMEM],
        out_specs=VMEM,
        scratch_shapes=[pltpu.SMEM((members,), I32)],
        compiler_params=LIMIT,
    )(block_owner, pressure)


def condense_kernel(incoming_ref, matrix_ref, slot_ref, offset_ref, out_ref, interior_ref, place_ref, place_smem, sem):
    slots, cases, rows = incoming_ref.shape
    most = matrix_ref.shape[1] // rows
    marks = incoming_ref[:, 0:16, :].astype(F32)[:, 0, 0:1]
    filled = (marks < EMPTY / 2).astype(F32)
    row, col = iota((slots, 128), 0), iota((slots, 128), 1)
    before = jnp.sum(jnp.where(row < col, filled, 0.0), axis=0, keepdims=True)
    here = jnp.sum(jnp.where(row == col, filled, 0.0), axis=0, keepdims=True)
    place = jnp.where(here > 0.5, before, float(most)).astype(I32)
    place_ref[...] = jnp.broadcast_to(place, place_ref.shape)
    copy = pltpu.make_async_copy(place_ref, place_smem, sem)
    copy.start()
    interior_ref[...] = jnp.zeros_like(interior_ref)
    copy.wait()
    for q in range(slots):
        at = pl.multiple_of(place_smem[0, q] * rows, rows)
        interior_ref[0:cases, pl.ds(at, rows)] = incoming_ref[q]
    boundary = dot_nt(matrix_ref[...], interior_ref[:, 0 : most * rows])
    lane = iota(boundary.shape, 1)
    with_offset = jnp.where(lane == cases, (offset_ref[...] + 1).astype(F32), boundary).astype(BF16)
    choose = (slot_ref[...] == iota((out_ref.shape[0], slot_ref.shape[1]), 0)).astype(F32).astype(BF16)
    out_ref[...] = jnp.dot(choose, with_offset, preferred_element_type=F32).astype(BF16)


def condense(incoming, matrix, slot, offset, members):
    slots, cases, rows = incoming.shape
    most = matrix.shape[1] // rows
    return pl.pallas_call(
        condense_kernel,
        out_shape=jax.ShapeDtypeStruct((members * RC, 128), BF16),
        in_specs=[VMEM] * 4,
        out_specs=VMEM,
        scratch_shapes=[
            pltpu.VMEM((128, (most + 1) * rows), BF16),
            pltpu.VMEM((8, 128), I32),
            pltpu.SMEM((8, 128), I32),
            pltpu.SemaphoreType.DMA,
        ],
        compiler_params=LIMIT,
    )(incoming, matrix, slot, offset)


def assemble_kernel(rows_ref, matrix_ref, root_ref, load_ref, out_ref):
    cases = load_ref.shape[0]
    groups = out_ref.shape[0]
    span = ROOT // groups
    rows = rows_ref[...]
    offsets = rows.astype(F32)[:, cases : cases + 1]
    hits = (offsets == (iota(rows.shape, 1) + 1).astype(F32)).astype(F32).astype(BF16)
    load = lax.dot_general(rows, hits, (((0,), (0,)), ((), ())), preferred_element_type=F32)[0:cases]
    load_ref[...] = load
    second = dot_nt(load.astype(BF16), matrix_ref[...]).astype(BF16)
    root = root_ref[...]
    for g in range(groups):
        out_ref[g, 0:cases, :] = second
        within = root - g * span
        index = jnp.where((within >= 0) & (within < span), within, 2 * span).astype(F32)
        out_ref[g, cases : cases + 16, :] = jnp.broadcast_to(index, (16, 128)).astype(BF16)


def assemble(rows, matrix, root, cases, groups):
    half = matrix.shape[1]
    return pl.pallas_call(
        assemble_kernel,
        out_shape=(
            jax.ShapeDtypeStruct((cases, half), F32),
            jax.ShapeDtypeStruct((groups, cases + 16, 128), BF16),
        ),
        in_specs=[VMEM] * 3,
        out_specs=(VMEM, VMEM),
        compiler_params=LIMIT,
    )(rows, matrix, root)


def root_kernel(parts_ref, out_ref):
    groups, depth, _ = parts_ref.shape
    cases = depth - 16
    span = out_ref.shape[0]
    want = iota((span, 128), 0).astype(F32)
    total = jnp.zeros(out_ref.shape, F32)
    for g in range(groups):
        index = parts_ref[g, cases : cases + 16, :].astype(F32)[0:1]
        hits = (want == index).astype(F32).astype(BF16)
        total += dot_nt(hits, parts_ref[g, 0:cases, :])
    out_ref[...] = total


def root_sum(parts, span, cases):
    return pl.pallas_call(
        root_kernel,
        out_shape=jax.ShapeDtypeStruct((span, cases), F32),
        in_specs=[VMEM],
        out_specs=VMEM,
        compiler_params=LIMIT,
    )(parts)


def exchange(x, axis):
    return lax.all_to_all(x, axis, split_axis=0, concat_axis=0, tiled=True)


def local(pressure, block_owner, level_one, level_one_map, level_two, level_two_map):
    members = lax.axis_size("se")
    groups = lax.axis_size("grp")
    member = lax.axis_index("se")
    cases, rows = pressure.shape[1:]
    half = level_two.shape[2]

    outgoing = pack(block_owner, pressure, members)
    incoming = exchange(outgoing, "se")

    target = level_one_map[0]
    dest = target // half
    dofs = jnp.arange(target.shape[0], dtype=I32)
    earlier = (dest[:, None] == dest[None, :]) & (dofs[:, None] < dofs[None, :])
    slot = dest * RC + jnp.sum(earlier.astype(I32), axis=0)
    offset = target - dest * half
    root = lax.dynamic_index_in_dim(level_two_map[0], member // 2, 0, keepdims=True)

    packed = condense(incoming, level_one[0], slot[None, :], offset[:, None], members)
    received = exchange(packed.reshape(members, RC, 128), "se").reshape(members * RC, 128)
    level_two_load, parts = assemble(received, level_two[0], root, cases, groups)
    parts = exchange(parts, "grp")
    span = ROOT // groups
    share = root_sum(parts, span, cases)
    share = exchange(share.reshape(members, span // members, cases), "se")
    root_load = jnp.sum(share, axis=0).T
    return (level_two_load[None], root_load)


def solution(mesh):
    placed = (
        P(("grp", "se"), None, None),
        P(("grp", "se")),
        P(("grp", "se"), None, None),
        P(("grp", "se"), None),
        P("grp", None, "se"),
        P("grp", None, None),
    )
    return jax.shard_map(
        local,
        mesh=mesh,
        in_specs=placed,
        out_specs=(P("grp", None, "se"), P(None, ("grp", "se"))),
        check_vma=False,
    )
```

```python
import jax
import jax.numpy as jnp
from jax import lax
from jax.experimental import pallas as pl
from jax.experimental.pallas import tpu as pltpu
from jax.sharding import PartitionSpec as P

ROOT = 4096
CAPACITY = 2
RC = 16
LANES = 128
EMPTY = 64.0
BF16 = jnp.bfloat16
F32 = jnp.float32
I32 = jnp.int32
VMEM = pl.BlockSpec(memory_space=pltpu.VMEM)
SMEM = pl.BlockSpec(memory_space=pltpu.SMEM)
ANY = pl.BlockSpec(memory_space=pl.ANY)
LIMIT = pltpu.CompilerParams(vmem_limit_bytes=16 * 1024 * 1024)


def iota(shape, dim):
    return lax.broadcasted_iota(I32, shape, dim)


def dot_nt(a, b):
    return lax.dot_general(a, b, (((1,), (1,)), ((), ())), preferred_element_type=F32)


def dot_tn(a, b):
    return lax.dot_general(a, b, (((0,), (0,)), ((), ())), preferred_element_type=F32)


def one_hot(hits):
    return hits.astype(F32).astype(BF16)


def pack_kernel(owner_ref, pressure_ref, out_ref, owner_smem, count_ref, mark_ref, owner_sem, mark_sem, block_sem):
    blocks = pressure_ref.shape[0]
    slots = out_ref.shape[0]
    owners = pltpu.make_async_copy(owner_ref, owner_smem, owner_sem)
    owners.start()
    mark_ref[...] = jnp.full(mark_ref.shape, EMPTY, BF16)
    marks = pltpu.make_async_copy(mark_ref, out_ref.at[:, 0:16, :], mark_sem)
    marks.start()
    for e in range(slots // CAPACITY):
        count_ref[e] = 0
    owners.wait()
    marks.wait()
    copies = []
    for t in range(blocks):
        owner = owner_smem[t]
        count = count_ref[owner]
        count_ref[owner] = count + 1
        copy = pltpu.make_async_copy(pressure_ref.at[t], out_ref.at[owner * CAPACITY + count], block_sem.at[t])
        copy.start()
        copies.append(copy)
    for copy in copies:
        copy.wait()


def pack(block_owner, pressure, members):
    blocks, cases, rows = pressure.shape
    return pl.pallas_call(
        pack_kernel,
        out_shape=jax.ShapeDtypeStruct((members * CAPACITY, cases, rows), BF16),
        in_specs=[ANY, ANY],
        out_specs=ANY,
        scratch_shapes=[
            pltpu.SMEM((blocks,), I32),
            pltpu.SMEM((members,), I32),
            pltpu.VMEM((members * CAPACITY, 16, rows), BF16),
            pltpu.SemaphoreType.DMA,
            pltpu.SemaphoreType.DMA,
            pltpu.SemaphoreType.DMA((blocks,)),
        ],
        compiler_params=pltpu.CompilerParams(vmem_limit_bytes=60 * 1024 * 1024),
    )(block_owner, pressure)


def plan_kernel(target_ref, matrix_ref, out_ref):
    out_ref[...] = target_ref[...]


def plan(target, matrix):
    return pl.pallas_call(
        plan_kernel,
        out_shape=jax.ShapeDtypeStruct(target.shape, I32),
        in_specs=[VMEM, ANY],
        out_specs=VMEM,
        compiler_params=LIMIT,
    )(target, matrix)


def condense_kernel(
    arrived_ref, matrix_ref, slot_ref, target_ref, out_ref, incoming_ref, interior_ref, place_ref, place_smem, sem, in_sem
):
    slots, cases, rows = incoming_ref.shape
    most = matrix_ref.shape[1] // rows
    heads = pltpu.make_async_copy(arrived_ref.at[:, 0:16, :], incoming_ref.at[:, 0:16, :], in_sem.at[0])
    tails = pltpu.make_async_copy(arrived_ref.at[:, 16:cases, :], incoming_ref.at[:, 16:cases, :], in_sem.at[1])
    heads.start()
    tails.start()
    heads.wait()
    marks = incoming_ref[:, 0:16, :].astype(F32)[:, 0, 0:1]
    filled = (marks < EMPTY / 2).astype(F32)
    row, col = iota((slots, LANES), 0), iota((slots, LANES), 1)
    before = jnp.sum(jnp.where(row < col, filled, 0.0), axis=0, keepdims=True)
    here = jnp.sum(jnp.where(row == col, filled, 0.0), axis=0, keepdims=True)
    place = jnp.where(here > 0.5, before, float(most)).astype(I32)
    place_ref[...] = jnp.broadcast_to(place, place_ref.shape)
    copy = pltpu.make_async_copy(place_ref, place_smem, sem)
    copy.start()
    interior_ref[...] = jnp.zeros_like(interior_ref)
    copy.wait()
    tails.wait()
    for q in range(slots):
        at = pl.multiple_of(place_smem[0, q] * rows, rows)
        interior_ref[0:cases, pl.ds(at, rows)] = incoming_ref[q]
    boundary = dot_nt(matrix_ref[...], interior_ref[:, 0 : most * rows])
    parts = cases // 2
    lane = iota(boundary.shape, 1)
    dest = target_ref[...] // rows
    offset = (target_ref[...] - dest * rows + 1).astype(F32)
    own = jnp.where(lane == cases + parts, offset, jnp.where(lane < cases, boundary, 0.0))
    lower = pltpu.roll(boundary, cases, 1)
    upper = pltpu.roll(boundary, parts, 1)
    other = jnp.where(dest % 2 == 1, lower, upper)
    other = jnp.where((lane >= cases) & (lane < cases + parts), other, 0.0)
    other = jnp.where(lane == cases + parts + 1, offset, other)
    slot = slot_ref[...]
    want = iota((out_ref.shape[0], slot.shape[1]), 0)
    sent = jnp.dot(one_hot(slot == want), own.astype(BF16), preferred_element_type=F32)
    sent += jnp.dot(one_hot(slot == want ^ RC), other.astype(BF16), preferred_element_type=F32)
    out_ref[...] = sent.astype(BF16)


def condense(incoming, matrix, slot, target, members):
    slots, cases, rows = incoming.shape
    depth = matrix.shape[1]
    return pl.pallas_call(
        condense_kernel,
        out_shape=jax.ShapeDtypeStruct((members * RC, LANES), BF16),
        in_specs=[ANY, VMEM, VMEM, VMEM],
        out_specs=VMEM,
        scratch_shapes=[
            pltpu.VMEM(incoming.shape, BF16),
            pltpu.VMEM((LANES, depth + rows), BF16),
            pltpu.VMEM((8, LANES), I32),
            pltpu.SMEM((8, LANES), I32),
            pltpu.SemaphoreType.DMA,
            pltpu.SemaphoreType.DMA((2,)),
        ],
        compiler_params=LIMIT,
    )(incoming, matrix, slot, target)


def assemble_kernel(side_ref, rows_ref, matrix_ref, other_ref, root_ref, load_ref, out_ref):
    cases = load_ref.shape[0]
    parts = cases // 2
    groups = out_ref.shape[0]
    span = ROOT // groups
    rows = rows_ref[...]
    offsets = rows.astype(F32)[:, cases + parts : cases + parts + 2]
    want = (iota(rows.shape, 1) + 1).astype(F32)
    load = dot_tn(rows, one_hot(offsets[:, 0:1] == want))[0:cases]
    other = dot_tn(rows, one_hot(offsets[:, 1:2] == want))[cases : cases + parts]
    load_ref[...] = load
    second = dot_nt(load.astype(BF16), matrix_ref[...])
    second = jnp.where(side_ref[0] == 0, second[0:parts], second[parts:cases])
    second = (second + dot_nt(other.astype(BF16), other_ref[...])).astype(BF16)
    root = root_ref[...]
    for g in range(groups):
        out_ref[g, 0:parts, :] = second
        within = root - g * span
        index = jnp.where((within >= 0) & (within < span), within, 2 * span).astype(F32)
        out_ref[g, parts : parts + 8, :] = jnp.broadcast_to(index, (8, LANES)).astype(BF16)


def assemble(side, rows, matrix, other, root, cases, groups):
    half = matrix.shape[1]
    return pl.pallas_call(
        assemble_kernel,
        out_shape=(
            jax.ShapeDtypeStruct((cases, half), F32),
            jax.ShapeDtypeStruct((groups, cases // 2 + 8, LANES), BF16),
        ),
        in_specs=[SMEM, VMEM, VMEM, VMEM, VMEM],
        out_specs=(VMEM, VMEM),
        compiler_params=LIMIT,
    )(side, rows, matrix, other, root)


def root_kernel(side_ref, parts_ref, out_ref):
    groups, depth, _ = parts_ref.shape
    parts = depth - 8
    span = out_ref.shape[0]
    want = iota((span, LANES), 0).astype(F32)
    total = jnp.zeros((span, parts), F32)
    for g in range(groups):
        index = parts_ref[g, parts:depth, :].astype(F32)[0:1]
        total += dot_nt(one_hot(want == index), parts_ref[g, 0:parts, :])
    zero = jnp.zeros_like(total)
    first = side_ref[0] == 0
    out_ref[:, 0:parts] = jnp.where(first, total, zero)
    out_ref[:, parts : 2 * parts] = jnp.where(first, zero, total)
    out_ref[:, 2 * parts :] = jnp.zeros((span, LANES - 2 * parts), F32)


def root_sum(side, parts, span):
    return pl.pallas_call(
        root_kernel,
        out_shape=jax.ShapeDtypeStruct((span, LANES), F32),
        in_specs=[SMEM, VMEM],
        out_specs=VMEM,
        compiler_params=LIMIT,
    )(side, parts)


def last_kernel(shares_ref, out_ref):
    total = shares_ref[0]
    for s in range(1, shares_ref.shape[0]):
        total += shares_ref[s]
    out_ref[...] = total[:, 0 : out_ref.shape[1]]


def last_sum(shares, cases):
    return pl.pallas_call(
        last_kernel,
        out_shape=jax.ShapeDtypeStruct((shares.shape[1], cases), F32),
        in_specs=[VMEM],
        out_specs=VMEM,
        compiler_params=LIMIT,
    )(shares)


def exchange(x, axis):
    return lax.all_to_all(x, axis, split_axis=0, concat_axis=0, tiled=True)


def local(pressure, block_owner, level_one, level_one_map, level_two, level_two_map):
    members = lax.axis_size("se")
    groups = lax.axis_size("grp")
    member = lax.axis_index("se")
    cases = pressure.shape[1]
    half = level_two.shape[2]

    outgoing = pack(block_owner, pressure, members)
    incoming = exchange(outgoing, "se")

    target = plan(level_one_map, level_one[0])[0]
    dest = target // half
    dofs = jnp.arange(target.shape[0], dtype=I32)
    earlier = (dest[:, None] == dest[None, :]) & (dofs[:, None] < dofs[None, :])
    slot = dest * RC + jnp.sum(earlier.astype(I32), axis=0)
    root = lax.dynamic_index_in_dim(level_two_map[0], member // 2, 0, keepdims=True)
    side = (member % 2)[None]
    partner = lax.ppermute(level_two[0], "se", [(i, i ^ 1) for i in range(members)])
    target, partner = lax.optimization_barrier((target, partner))

    packed = condense(incoming, level_one[0], slot[None, :], target[:, None], members)
    received = exchange(packed.reshape(members, RC, LANES), "se").reshape(members * RC, LANES)
    level_two_load, parts = assemble(side, received, level_two[0], partner, root, cases, groups)
    parts = exchange(parts, "grp")
    span = ROOT // groups
    share = root_sum(side, parts, span)
    share = exchange(share.reshape(members, span // members, LANES), "se")
    root_load = last_sum(share, cases).T
    return (level_two_load[None], root_load)


def solution(mesh):
    placed = (
        P(("grp", "se"), None, None),
        P(("grp", "se")),
        P(("grp", "se"), None, None),
        P(("grp", "se"), None),
        P("grp", None, "se"),
        P("grp", None, None),
    )
    return jax.shard_map(
        local,
        mesh=mesh,
        in_specs=placed,
        out_specs=(P("grp", None, "se"), P(None, ("grp", "se"))),
        check_vma=False,
    )
```

```python
import jax
import jax.numpy as jnp
from jax import lax
from jax.experimental import pallas as pl
from jax.experimental.pallas import tpu as pltpu
from jax.sharding import PartitionSpec as P

ROOT = 4096
CAPACITY = 2
RC = 16
LANES = 128
CHUNKS = 4
EMPTY = 64.0
BF16 = jnp.bfloat16
F32 = jnp.float32
I32 = jnp.int32
VMEM = pl.BlockSpec(memory_space=pltpu.VMEM)
SMEM = pl.BlockSpec(memory_space=pltpu.SMEM)
ANY = pl.BlockSpec(memory_space=pl.ANY)
WIDE = pltpu.CompilerParams(vmem_limit_bytes=62 * 1024 * 1024)
ROOMY = pltpu.CompilerParams(vmem_limit_bytes=52 * 1024 * 1024)
LIMIT = pltpu.CompilerParams(vmem_limit_bytes=16 * 1024 * 1024)


def iota(shape, dim):
    return lax.broadcasted_iota(I32, shape, dim)


def dot_nt(a, b):
    return lax.dot_general(a, b, (((1,), (1,)), ((), ())), preferred_element_type=F32)


def dot_tn(a, b):
    return lax.dot_general(a, b, (((0,), (0,)), ((), ())), preferred_element_type=F32)


def one_hot(hits):
    return hits.astype(F32).astype(BF16)


def pack_kernel(owner_ref, pressure_ref, out_ref, held_ref, owner_smem, count_ref, owner_sem, block_sem):
    slots = out_ref.shape[0]
    owners = pltpu.make_async_copy(owner_ref, owner_smem, owner_sem)
    blocks = pltpu.make_async_copy(pressure_ref, held_ref, block_sem)
    owners.start()
    blocks.start()
    out_ref[:, 0:16, :] = jnp.full((slots, 16, out_ref.shape[2]), EMPTY, BF16)
    for e in range(slots // CAPACITY):
        count_ref[e] = 0
    owners.wait()
    blocks.wait()
    for t in range(held_ref.shape[0]):
        owner = owner_smem[t]
        count = count_ref[owner]
        count_ref[owner] = count + 1
        out_ref[owner * CAPACITY + count] = held_ref[t]


def pack(block_owner, pressure, members):
    blocks, cases, rows = pressure.shape
    return pl.pallas_call(
        pack_kernel,
        out_shape=jax.ShapeDtypeStruct((members * CAPACITY, cases, rows), BF16),
        in_specs=[ANY, ANY],
        out_specs=VMEM,
        scratch_shapes=[
            pltpu.VMEM((blocks, cases, rows), BF16),
            pltpu.SMEM((blocks,), I32),
            pltpu.SMEM((members,), I32),
            pltpu.SemaphoreType.DMA,
            pltpu.SemaphoreType.DMA,
        ],
        compiler_params=WIDE,
    )(block_owner, pressure)


def condense_kernel(
    incoming_ref, level_ref, slot_ref, target_ref, out_ref, matrix_ref, interior_ref, level_sem
):
    slots, cases, rows = incoming_ref.shape
    most = matrix_ref.shape[1] // rows
    width = most * rows // CHUNKS
    chunks = []
    for c in range(CHUNKS):
        part = (slice(None), slice(c * width, (c + 1) * width))
        chunks.append(pltpu.make_async_copy(level_ref.at[part], matrix_ref.at[part], level_sem.at[c]))
        chunks[c].start()
    interior_ref[...] = jnp.zeros_like(interior_ref)
    marks = incoming_ref[:, 0:16, :].astype(F32)[:, 0, 0:1]
    filled = (marks < EMPTY / 2).astype(F32)
    row, col = iota((slots, LANES), 0), iota((slots, LANES), 1)
    before = jnp.sum(jnp.where(row < col, filled, 0.0), axis=0, keepdims=True)
    here = jnp.sum(jnp.where(row == col, filled, 0.0), axis=0, keepdims=True)
    place = jnp.where(here > 0.5, before, float(most)).astype(I32) * rows
    for q in range(slots):
        at = pl.multiple_of(place[0, q], rows)
        interior_ref[0:cases, pl.ds(at, rows)] = incoming_ref[q]
    boundary = jnp.zeros((matrix_ref.shape[0], LANES), F32)
    for c in range(CHUNKS):
        chunks[c].wait()
        span = slice(c * width, (c + 1) * width)
        boundary += dot_nt(matrix_ref[:, span], interior_ref[:, span])
    parts = cases // 2
    lane = iota(boundary.shape, 1)
    dest = target_ref[...] // rows
    offset = (target_ref[...] - dest * rows + 1).astype(F32)
    own = jnp.where(lane == cases + parts, offset, jnp.where(lane < cases, boundary, 0.0))
    lower = pltpu.roll(boundary, cases, 1)
    upper = pltpu.roll(boundary, parts, 1)
    other = jnp.where(dest % 2 == 1, lower, upper)
    other = jnp.where((lane >= cases) & (lane < cases + parts), other, 0.0)
    other = jnp.where(lane == cases + parts + 1, offset, other)
    slot = slot_ref[...]
    want = iota((out_ref.shape[0], slot.shape[1]), 0)
    sent = jnp.dot(one_hot(slot == want), own.astype(BF16), preferred_element_type=F32)
    sent += jnp.dot(one_hot(slot == want ^ RC), other.astype(BF16), preferred_element_type=F32)
    out_ref[...] = sent.astype(BF16)


def condense(incoming, matrix, slot, target, members):
    depth = matrix.shape[1]
    rows = incoming.shape[2]
    return pl.pallas_call(
        condense_kernel,
        out_shape=jax.ShapeDtypeStruct((members * RC, LANES), BF16),
        in_specs=[VMEM, ANY, VMEM, VMEM],
        out_specs=VMEM,
        scratch_shapes=[
            pltpu.VMEM(matrix.shape, BF16),
            pltpu.VMEM((LANES, depth + rows), BF16),
            pltpu.SemaphoreType.DMA((CHUNKS,)),
        ],
        compiler_params=ROOMY,
    )(incoming, matrix, slot, target)


def assemble_kernel(side_ref, rows_ref, matrix_ref, other_ref, root_ref, load_ref, out_ref):
    cases = load_ref.shape[0]
    parts = cases // 2
    groups = out_ref.shape[0]
    span = ROOT // groups
    rows = rows_ref[...]
    offsets = rows.astype(F32)[:, cases + parts : cases + parts + 2]
    want = (iota(rows.shape, 1) + 1).astype(F32)
    load = dot_tn(rows, one_hot(offsets[:, 0:1] == want))[0:cases]
    other = dot_tn(rows, one_hot(offsets[:, 1:2] == want))[cases : cases + parts]
    load_ref[...] = load
    second = dot_nt(load.astype(BF16), matrix_ref[...])
    second = jnp.where(side_ref[0] == 0, second[0:parts], second[parts:cases])
    second = (second + dot_nt(other.astype(BF16), other_ref[...])).astype(BF16)
    root = root_ref[...]
    for g in range(groups):
        out_ref[g, 0:parts, :] = second
        within = root - g * span
        index = jnp.where((within >= 0) & (within < span), within, 2 * span).astype(F32)
        out_ref[g, parts : parts + 8, :] = jnp.broadcast_to(index, (8, LANES)).astype(BF16)


def assemble(side, rows, matrix, other, root, cases, groups):
    half = matrix.shape[1]
    return pl.pallas_call(
        assemble_kernel,
        out_shape=(
            jax.ShapeDtypeStruct((cases, half), F32),
            jax.ShapeDtypeStruct((groups, cases // 2 + 8, LANES), BF16),
        ),
        in_specs=[SMEM, VMEM, VMEM, VMEM, VMEM],
        out_specs=(VMEM, VMEM),
        compiler_params=LIMIT,
    )(side, rows, matrix, other, root)


def root_kernel(side_ref, parts_ref, out_ref):
    groups, depth, _ = parts_ref.shape
    parts = depth - 8
    span = out_ref.shape[0]
    want = iota((span, LANES), 0).astype(F32)
    total = jnp.zeros((span, parts), F32)
    for g in range(groups):
        index = parts_ref[g, parts:depth, :].astype(F32)[0:1]
        total += dot_nt(one_hot(want == index), parts_ref[g, 0:parts, :])
    zero = jnp.zeros_like(total)
    first = side_ref[0] == 0
    out_ref[:, 0:parts] = jnp.where(first, total, zero)
    out_ref[:, parts : 2 * parts] = jnp.where(first, zero, total)
    out_ref[:, 2 * parts :] = jnp.zeros((span, LANES - 2 * parts), F32)


def root_sum(side, parts, span):
    return pl.pallas_call(
        root_kernel,
        out_shape=jax.ShapeDtypeStruct((span, LANES), F32),
        in_specs=[SMEM, VMEM],
        out_specs=VMEM,
        compiler_params=LIMIT,
    )(side, parts)


def last_kernel(shares_ref, out_ref):
    total = shares_ref[0]
    for s in range(1, shares_ref.shape[0]):
        total += shares_ref[s]
    out_ref[...] = total[:, 0 : out_ref.shape[1]]


def last_sum(shares, cases):
    return pl.pallas_call(
        last_kernel,
        out_shape=jax.ShapeDtypeStruct((shares.shape[1], cases), F32),
        in_specs=[VMEM],
        out_specs=VMEM,
        compiler_params=LIMIT,
    )(shares)


def exchange(x, axis):
    return lax.all_to_all(x, axis, split_axis=0, concat_axis=0, tiled=True)


def local(pressure, block_owner, level_one, level_one_map, level_two, level_two_map):
    members = lax.axis_size("se")
    groups = lax.axis_size("grp")
    member = lax.axis_index("se")
    cases = pressure.shape[1]
    half = level_two.shape[2]

    outgoing = pack(block_owner, pressure, members)
    incoming = exchange(outgoing, "se")

    target = level_one_map[0]
    dest = target // half
    dofs = jnp.arange(target.shape[0], dtype=I32)
    earlier = (dest[:, None] == dest[None, :]) & (dofs[:, None] < dofs[None, :])
    slot = dest * RC + jnp.sum(earlier.astype(I32), axis=0)
    root = lax.dynamic_index_in_dim(level_two_map[0], member // 2, 0, keepdims=True)
    side = (member % 2)[None]
    partner = lax.ppermute(level_two[0], "se", [(i, i ^ 1) for i in range(members)])
    target, partner = lax.optimization_barrier((target, partner))

    packed = condense(incoming, level_one[0], slot[None, :], target[:, None], members)
    received = exchange(packed.reshape(members, RC, LANES), "se").reshape(members * RC, LANES)
    level_two_load, parts = assemble(side, received, level_two[0], partner, root, cases, groups)
    parts = exchange(parts, "grp")
    span = ROOT // groups
    share = root_sum(side, parts, span)
    share = exchange(share.reshape(members, span // members, LANES), "se")
    root_load = last_sum(share, cases).T
    return (level_two_load[None], root_load)


def solution(mesh):
    placed = (
        P(("grp", "se"), None, None),
        P(("grp", "se")),
        P(("grp", "se"), None, None),
        P(("grp", "se"), None),
        P("grp", None, "se"),
        P("grp", None, None),
    )
    return jax.shard_map(
        local,
        mesh=mesh,
        in_specs=placed,
        out_specs=(P("grp", None, "se"), P(None, ("grp", "se"))),
        check_vma=False,
    )
```

```python
import jax
import jax.numpy as jnp
from jax import lax
from jax.experimental import pallas as pl
from jax.experimental.pallas import tpu as pltpu
from jax.sharding import PartitionSpec as P

ROOT = 4096
CAPACITY = 2
RC = 16
LANES = 128
EMPTY = 64.0
BF16 = jnp.bfloat16
F32 = jnp.float32
I32 = jnp.int32
VMEM = pl.BlockSpec(memory_space=pltpu.VMEM)
SMEM = pl.BlockSpec(memory_space=pltpu.SMEM)
ANY = pl.BlockSpec(memory_space=pl.ANY)
WIDE = pltpu.CompilerParams(vmem_limit_bytes=60 * 1024 * 1024)
ROOMY = pltpu.CompilerParams(vmem_limit_bytes=16 * 1024 * 1024)
LIMIT = pltpu.CompilerParams(vmem_limit_bytes=16 * 1024 * 1024)


def iota(shape, dim):
    return lax.broadcasted_iota(I32, shape, dim)


def dot_nt(a, b):
    return lax.dot_general(a, b, (((1,), (1,)), ((), ())), preferred_element_type=F32)


def dot_tn(a, b):
    return lax.dot_general(a, b, (((0,), (0,)), ((), ())), preferred_element_type=F32)


def one_hot(hits):
    return hits.astype(F32).astype(BF16)


def pack_kernel(owner_ref, pressure_ref, out_ref, held_ref, owner_smem, count_ref, owner_sem, block_sem):
    slots = out_ref.shape[0]
    owners = pltpu.make_async_copy(owner_ref, owner_smem, owner_sem)
    blocks = pltpu.make_async_copy(pressure_ref, held_ref, block_sem)
    owners.start()
    blocks.start()
    out_ref[:, 0:16, :] = jnp.full((slots, 16, out_ref.shape[2]), EMPTY, BF16)
    for e in range(slots // CAPACITY):
        count_ref[e] = 0
    owners.wait()
    blocks.wait()
    for t in range(held_ref.shape[0]):
        owner = owner_smem[t]
        count = count_ref[owner]
        count_ref[owner] = count + 1
        out_ref[owner * CAPACITY + count] = held_ref[t]


def pack(block_owner, pressure, members):
    blocks, cases, rows = pressure.shape
    return pl.pallas_call(
        pack_kernel,
        out_shape=jax.ShapeDtypeStruct((members * CAPACITY, cases, rows), BF16),
        in_specs=[ANY, ANY],
        out_specs=VMEM,
        scratch_shapes=[
            pltpu.VMEM((blocks, cases, rows), BF16),
            pltpu.SMEM((blocks,), I32),
            pltpu.SMEM((members,), I32),
            pltpu.SemaphoreType.DMA,
            pltpu.SemaphoreType.DMA,
        ],
        compiler_params=WIDE,
    )(block_owner, pressure)


def plan_kernel(target_ref, matrix_ref, out_ref):
    out_ref[...] = target_ref[...]


def plan(target, matrix):
    return pl.pallas_call(
        plan_kernel,
        out_shape=jax.ShapeDtypeStruct(target.shape, I32),
        in_specs=[VMEM, ANY],
        out_specs=VMEM,
        compiler_params=pltpu.CompilerParams(vmem_limit_bytes=16 * 1024 * 1024),
    )(target, matrix)


def condense_kernel(
    arrived_ref, matrix_ref, slot_ref, target_ref, out_ref, incoming_ref, interior_ref, in_sem
):
    slots, cases, rows = incoming_ref.shape
    most = matrix_ref.shape[1] // rows
    arriving = pltpu.make_async_copy(arrived_ref, incoming_ref, in_sem)
    arriving.start()
    interior_ref[...] = jnp.zeros_like(interior_ref)
    arriving.wait()
    marks = incoming_ref[:, 0:16, :].astype(F32)[:, 0, 0:1]
    filled = (marks < EMPTY / 2).astype(F32)
    row, col = iota((slots, LANES), 0), iota((slots, LANES), 1)
    before = jnp.sum(jnp.where(row < col, filled, 0.0), axis=0, keepdims=True)
    here = jnp.sum(jnp.where(row == col, filled, 0.0), axis=0, keepdims=True)
    place = jnp.where(here > 0.5, before, float(most)).astype(I32) * rows
    for q in range(slots):
        at = pl.multiple_of(place[0, q], rows)
        interior_ref[0:cases, pl.ds(at, rows)] = incoming_ref[q]
    boundary = dot_nt(matrix_ref[...], interior_ref[:, 0 : most * rows])
    parts = cases // 2
    lane = iota(boundary.shape, 1)
    dest = target_ref[...] // rows
    offset = (target_ref[...] - dest * rows + 1).astype(F32)
    own = jnp.where(lane == cases + parts, offset, jnp.where(lane < cases, boundary, 0.0))
    lower = pltpu.roll(boundary, cases, 1)
    upper = pltpu.roll(boundary, parts, 1)
    other = jnp.where(dest % 2 == 1, lower, upper)
    other = jnp.where((lane >= cases) & (lane < cases + parts), other, 0.0)
    other = jnp.where(lane == cases + parts + 1, offset, other)
    slot = slot_ref[...]
    want = iota((out_ref.shape[0], slot.shape[1]), 0)
    sent = jnp.dot(one_hot(slot == want), own.astype(BF16), preferred_element_type=F32)
    sent += jnp.dot(one_hot(slot == want ^ RC), other.astype(BF16), preferred_element_type=F32)
    out_ref[...] = sent.astype(BF16)


def condense(incoming, matrix, slot, target, members):
    depth = matrix.shape[1]
    rows = incoming.shape[2]
    return pl.pallas_call(
        condense_kernel,
        out_shape=jax.ShapeDtypeStruct((members * RC, LANES), BF16),
        in_specs=[ANY, VMEM, VMEM, VMEM],
        out_specs=VMEM,
        scratch_shapes=[
            pltpu.VMEM(incoming.shape, BF16),
            pltpu.VMEM((LANES, depth + rows), BF16),
            pltpu.SemaphoreType.DMA,
        ],
        compiler_params=ROOMY,
    )(incoming, matrix, slot, target)


def assemble_kernel(side_ref, rows_ref, matrix_ref, other_ref, root_ref, load_ref, out_ref):
    cases = load_ref.shape[0]
    parts = cases // 2
    groups = out_ref.shape[0]
    span = ROOT // groups
    rows = rows_ref[...]
    offsets = rows.astype(F32)[:, cases + parts : cases + parts + 2]
    want = (iota(rows.shape, 1) + 1).astype(F32)
    load = dot_tn(rows, one_hot(offsets[:, 0:1] == want))[0:cases]
    other = dot_tn(rows, one_hot(offsets[:, 1:2] == want))[cases : cases + parts]
    load_ref[...] = load
    second = dot_nt(load.astype(BF16), matrix_ref[...])
    second = jnp.where(side_ref[0] == 0, second[0:parts], second[parts:cases])
    second = (second + dot_nt(other.astype(BF16), other_ref[...])).astype(BF16)
    root = root_ref[...]
    for g in range(groups):
        out_ref[g, 0:parts, :] = second
        within = root - g * span
        index = jnp.where((within >= 0) & (within < span), within, 2 * span).astype(F32)
        out_ref[g, parts : parts + 8, :] = jnp.broadcast_to(index, (8, LANES)).astype(BF16)


def assemble(side, rows, matrix, other, root, cases, groups):
    half = matrix.shape[1]
    return pl.pallas_call(
        assemble_kernel,
        out_shape=(
            jax.ShapeDtypeStruct((cases, half), F32),
            jax.ShapeDtypeStruct((groups, cases // 2 + 8, LANES), BF16),
        ),
        in_specs=[SMEM, VMEM, VMEM, VMEM, VMEM],
        out_specs=(VMEM, VMEM),
        compiler_params=LIMIT,
    )(side, rows, matrix, other, root)


def root_kernel(side_ref, parts_ref, out_ref):
    groups, depth, _ = parts_ref.shape
    parts = depth - 8
    span = out_ref.shape[0]
    want = iota((span, LANES), 0).astype(F32)
    total = jnp.zeros((span, parts), F32)
    for g in range(groups):
        index = parts_ref[g, parts:depth, :].astype(F32)[0:1]
        total += dot_nt(one_hot(want == index), parts_ref[g, 0:parts, :])
    zero = jnp.zeros_like(total)
    first = side_ref[0] == 0
    out_ref[:, 0:parts] = jnp.where(first, total, zero)
    out_ref[:, parts : 2 * parts] = jnp.where(first, zero, total)
    out_ref[:, 2 * parts :] = jnp.zeros((span, LANES - 2 * parts), F32)


def root_sum(side, parts, span):
    return pl.pallas_call(
        root_kernel,
        out_shape=jax.ShapeDtypeStruct((span, LANES), F32),
        in_specs=[SMEM, VMEM],
        out_specs=VMEM,
        compiler_params=LIMIT,
    )(side, parts)


def last_kernel(shares_ref, out_ref):
    total = shares_ref[0]
    for s in range(1, shares_ref.shape[0]):
        total += shares_ref[s]
    out_ref[...] = total[:, 0 : out_ref.shape[1]]


def last_sum(shares, cases):
    return pl.pallas_call(
        last_kernel,
        out_shape=jax.ShapeDtypeStruct((shares.shape[1], cases), F32),
        in_specs=[VMEM],
        out_specs=VMEM,
        compiler_params=LIMIT,
    )(shares)


def exchange(x, axis):
    return lax.all_to_all(x, axis, split_axis=0, concat_axis=0, tiled=True)


def local(pressure, block_owner, level_one, level_one_map, level_two, level_two_map):
    members = lax.axis_size("se")
    groups = lax.axis_size("grp")
    member = lax.axis_index("se")
    cases = pressure.shape[1]
    half = level_two.shape[2]

    outgoing = pack(block_owner, pressure, members)
    incoming = exchange(outgoing, "se")

    target = plan(level_one_map, level_one[0])[0]
    dest = target // half
    dofs = jnp.arange(target.shape[0], dtype=I32)
    earlier = (dest[:, None] == dest[None, :]) & (dofs[:, None] < dofs[None, :])
    slot = dest * RC + jnp.sum(earlier.astype(I32), axis=0)
    root = lax.dynamic_index_in_dim(level_two_map[0], member // 2, 0, keepdims=True)
    side = (member % 2)[None]
    partner = lax.ppermute(level_two[0], "se", [(i, i ^ 1) for i in range(members)])
    target, partner = lax.optimization_barrier((target, partner))

    packed = condense(incoming, level_one[0], slot[None, :], target[:, None], members)
    received = exchange(packed.reshape(members, RC, LANES), "se").reshape(members * RC, LANES)
    level_two_load, parts = assemble(side, received, level_two[0], partner, root, cases, groups)
    parts = exchange(parts, "grp")
    span = ROOT // groups
    share = root_sum(side, parts, span)
    share = exchange(share.reshape(members, span // members, LANES), "se")
    root_load = last_sum(share, cases).T
    return (level_two_load[None], root_load)


def solution(mesh):
    placed = (
        P(("grp", "se"), None, None),
        P(("grp", "se")),
        P(("grp", "se"), None, None),
        P(("grp", "se"), None),
        P("grp", None, "se"),
        P("grp", None, None),
    )
    return jax.shard_map(
        local,
        mesh=mesh,
        in_specs=placed,
        out_specs=(P("grp", None, "se"), P(None, ("grp", "se"))),
        check_vma=False,
    )
```

```python
import jax
import jax.numpy as jnp
from jax import lax
from jax.experimental import pallas as pl
from jax.experimental.pallas import tpu as pltpu
from jax.sharding import PartitionSpec as P

ROOT = 4096
CAPACITY = 2
RC = 16
LANES = 128
EMPTY = 64.0
BF16 = jnp.bfloat16
F32 = jnp.float32
I32 = jnp.int32
VMEM = pl.BlockSpec(memory_space=pltpu.VMEM)
SMEM = pl.BlockSpec(memory_space=pltpu.SMEM)
ANY = pl.BlockSpec(memory_space=pl.ANY)
WIDE = pltpu.CompilerParams(vmem_limit_bytes=60 * 1024 * 1024)
ROOMY = pltpu.CompilerParams(vmem_limit_bytes=16 * 1024 * 1024)
LIMIT = pltpu.CompilerParams(vmem_limit_bytes=16 * 1024 * 1024)


def iota(shape, dim):
    return lax.broadcasted_iota(I32, shape, dim)


def dot_nt(a, b):
    return lax.dot_general(a, b, (((1,), (1,)), ((), ())), preferred_element_type=F32)


def dot_tn(a, b):
    return lax.dot_general(a, b, (((0,), (0,)), ((), ())), preferred_element_type=F32)


def one_hot(hits):
    return hits.astype(F32).astype(BF16)


def pack_kernel(owner_ref, pressure_ref, out_ref, held_ref, owner_smem, count_ref, owner_sem, block_sem):
    slots = out_ref.shape[0]
    owners = pltpu.make_async_copy(owner_ref, owner_smem, owner_sem)
    blocks = pltpu.make_async_copy(pressure_ref, held_ref, block_sem)
    owners.start()
    blocks.start()
    out_ref[:, 0:16, :] = jnp.full((slots, 16, out_ref.shape[2]), EMPTY, BF16)
    for e in range(slots // CAPACITY):
        count_ref[e] = 0
    owners.wait()
    blocks.wait()
    for t in range(held_ref.shape[0]):
        owner = owner_smem[t]
        count = count_ref[owner]
        count_ref[owner] = count + 1
        out_ref[owner * CAPACITY + count] = held_ref[t]


def pack(block_owner, pressure, members):
    blocks, cases, rows = pressure.shape
    return pl.pallas_call(
        pack_kernel,
        out_shape=jax.ShapeDtypeStruct((members * CAPACITY, cases, rows), BF16),
        in_specs=[ANY, ANY],
        out_specs=VMEM,
        scratch_shapes=[
            pltpu.VMEM((blocks, cases, rows), BF16),
            pltpu.SMEM((blocks,), I32),
            pltpu.SMEM((members,), I32),
            pltpu.SemaphoreType.DMA,
            pltpu.SemaphoreType.DMA,
        ],
        compiler_params=WIDE,
    )(block_owner, pressure)


def plan_kernel(target_ref, matrix_ref, out_ref):
    out_ref[...] = target_ref[...]


def plan(target, matrix):
    return pl.pallas_call(
        plan_kernel,
        out_shape=jax.ShapeDtypeStruct(target.shape, I32),
        in_specs=[VMEM, ANY],
        out_specs=VMEM,
        compiler_params=pltpu.CompilerParams(vmem_limit_bytes=16 * 1024 * 1024),
    )(target, matrix)


def condense_kernel(
    arrived_ref, matrix_ref, slot_ref, target_ref, out_ref, incoming_ref, interior_ref, in_sem
):
    slots, cases, rows = incoming_ref.shape
    most = matrix_ref.shape[1] // rows
    arriving = pltpu.make_async_copy(arrived_ref, incoming_ref, in_sem)
    arriving.start()
    interior_ref[...] = jnp.zeros_like(interior_ref)
    arriving.wait()
    marks = incoming_ref[:, 0:16, :].astype(F32)[:, 0, 0:1]
    filled = (marks < EMPTY / 2).astype(F32)
    row, col = iota((slots, LANES), 0), iota((slots, LANES), 1)
    before = jnp.sum(jnp.where(row < col, filled, 0.0), axis=0, keepdims=True)
    here = jnp.sum(jnp.where(row == col, filled, 0.0), axis=0, keepdims=True)
    place = jnp.where(here > 0.5, before, float(most)).astype(I32) * rows
    for q in range(slots):
        at = pl.multiple_of(place[0, q], rows)
        interior_ref[0:cases, pl.ds(at, rows)] = incoming_ref[q]
    boundary = dot_nt(matrix_ref[...], interior_ref[:, 0 : most * rows])
    parts = cases // 2
    lane = iota(boundary.shape, 1)
    dest = target_ref[...] // rows
    offset = (target_ref[...] - dest * rows + 1).astype(F32)
    own = jnp.where(lane == cases + parts, offset, jnp.where(lane < cases, boundary, 0.0))
    lower = pltpu.roll(boundary, cases, 1)
    upper = pltpu.roll(boundary, parts, 1)
    other = jnp.where(dest % 2 == 1, lower, upper)
    other = jnp.where((lane >= cases) & (lane < cases + parts), other, 0.0)
    other = jnp.where(lane == cases + parts + 1, offset, other)
    slot = slot_ref[...]
    want = iota((out_ref.shape[0], slot.shape[1]), 0)
    sent = jnp.dot(one_hot(slot == want), own.astype(BF16), preferred_element_type=F32)
    sent += jnp.dot(one_hot(slot == want ^ RC), other.astype(BF16), preferred_element_type=F32)
    out_ref[...] = sent.astype(BF16)


def condense(incoming, matrix, slot, target, members):
    depth = matrix.shape[1]
    rows = incoming.shape[2]
    return pl.pallas_call(
        condense_kernel,
        out_shape=jax.ShapeDtypeStruct((members * RC, LANES), BF16),
        in_specs=[ANY, VMEM, VMEM, VMEM],
        out_specs=VMEM,
        scratch_shapes=[
            pltpu.VMEM(incoming.shape, BF16),
            pltpu.VMEM((LANES, depth + rows), BF16),
            pltpu.SemaphoreType.DMA,
        ],
        compiler_params=ROOMY,
    )(incoming, matrix, slot, target)


def assemble_kernel(side_ref, rows_ref, matrix_ref, other_ref, load_ref, out_ref):
    cases = load_ref.shape[0]
    parts = cases // 2
    rows = rows_ref[...]
    offsets = rows.astype(F32)[:, cases + parts : cases + parts + 2]
    want = (iota(rows.shape, 1) + 1).astype(F32)
    load = dot_tn(rows, one_hot(offsets[:, 0:1] == want))[0:cases]
    other = dot_tn(rows, one_hot(offsets[:, 1:2] == want))[cases : cases + parts]
    load_ref[...] = load
    second = dot_nt(load.astype(BF16), matrix_ref[...])
    second = jnp.where(side_ref[0] == 0, second[0:parts], second[parts:cases])
    out_ref[...] = (second + dot_nt(other.astype(BF16), other_ref[...])).astype(BF16)


def assemble(side, rows, matrix, other, cases):
    half = matrix.shape[1]
    return pl.pallas_call(
        assemble_kernel,
        out_shape=(
            jax.ShapeDtypeStruct((cases, half), F32),
            jax.ShapeDtypeStruct((cases // 2, LANES), BF16),
        ),
        in_specs=[SMEM, VMEM, VMEM, VMEM],
        out_specs=(VMEM, VMEM),
        compiler_params=LIMIT,
    )(side, rows, matrix, other)


def root_kernel(key_ref, mine_ref, theirs_ref, out_ref):
    rows = out_ref.shape[0]
    parts = mine_ref.shape[0]
    share = LANES // parts
    row = iota((rows, LANES), 0)
    both = jnp.concatenate([mine_ref[...], theirs_ref[...]], axis=1)
    zero = jnp.zeros_like(both)
    total = jnp.zeros(out_ref.shape, F32)
    for k in range(share):
        hits = [one_hot(row * share + k == key_ref[c : c + 1, :]) for c in range(2)]
        placed = jnp.concatenate([both if j == k else zero for j in range(share)], axis=0)
        total += dot_nt(jnp.concatenate(hits, axis=1), placed)
    out_ref[...] = total.astype(BF16)


def root_sum(key, mine, theirs, rows):
    return pl.pallas_call(
        root_kernel,
        out_shape=jax.ShapeDtypeStruct((rows, LANES), BF16),
        in_specs=[VMEM, VMEM, VMEM],
        out_specs=VMEM,
        compiler_params=LIMIT,
    )(key, mine, theirs)


def last_kernel(shares_ref, out_ref):
    columns, cases = out_ref.shape
    parts = cases // 2
    share = LANES // parts
    each = columns // share
    period = 2 * each
    total = jnp.zeros((16, LANES), F32)
    for s in range(shares_ref.shape[0] // 16):
        total += shares_ref[16 * s : 16 * s + 16, :].astype(F32)
    halves = total[0:period]
    for s in range(1, 16 // period):
        halves += total[s * period : (s + 1) * period]
    for k in range(share):
        lanes = halves[:, k * parts : (k + 1) * parts]
        both = jnp.concatenate([lanes[0:each], lanes[each:period]], axis=1)
        for i in range(each):
            out_ref[i * share + k : i * share + k + 1, :] = both[i : i + 1]


def last_sum(shares, columns, cases):
    return pl.pallas_call(
        last_kernel,
        out_shape=jax.ShapeDtypeStruct((columns, cases), F32),
        in_specs=[VMEM],
        out_specs=VMEM,
        compiler_params=LIMIT,
    )(shares)


def exchange(x, axis):
    return lax.all_to_all(x, axis, split_axis=0, concat_axis=0, tiled=True)


def local(pressure, block_owner, level_one, level_one_map, level_two, level_two_map):
    members = lax.axis_size("se")
    groups = lax.axis_size("y") * lax.axis_size("core")
    core = lax.axis_index("core")
    member = lax.axis_index("se")
    cases = pressure.shape[1]
    half = level_two.shape[2]

    outgoing = pack(block_owner, pressure, members)
    incoming = exchange(outgoing, "se")

    target = plan(level_one_map, level_one[0])[0]
    dest = target // half
    dofs = jnp.arange(target.shape[0], dtype=I32)
    earlier = (dest[:, None] == dest[None, :]) & (dofs[:, None] < dofs[None, :])
    slot = dest * RC + jnp.sum(earlier.astype(I32), axis=0)
    root = lax.dynamic_index_in_dim(level_two_map[0], member // 2, 0, keepdims=True)
    side = (member % 2)[None]
    partner = lax.ppermute(level_two[0], "se", [(i, i ^ 1) for i in range(members)])
    span = ROOT // groups
    roots = jnp.concatenate([root, lax.ppermute(root, "core", [(0, 1), (1, 0)])], axis=0)
    group = roots // span
    key = jnp.where(group % 2 == core, group // 2 * span + roots % span, -1)
    target, partner, key = lax.optimization_barrier((target, partner, key))

    packed = condense(incoming, level_one[0], slot[None, :], target[:, None], members)
    received = exchange(packed.reshape(members, RC, LANES), "se").reshape(members * RC, LANES)
    level_two_load, second = assemble(side, received, level_two[0], partner, cases)
    theirs = lax.ppermute(second, "core", [(0, 1), (1, 0)])
    columns = span // members
    share = root_sum(key, second, theirs, groups // 2 * span * (cases // 2) // LANES)
    share = exchange(share, ("y", "se"))
    root_load = last_sum(share, columns, cases).T
    return (level_two_load[None], root_load)


def solution(mesh):
    groups, members = mesh.devices.shape
    split = jax.sharding.Mesh(mesh.devices.reshape(groups // 2, 2, members), ("y", "core", "se"))
    grp = ("y", "core")
    every = ("y", "core", "se")
    placed = (
        P(every, None, None),
        P(every),
        P(every, None, None),
        P(every, None),
        P(grp, None, "se"),
        P(grp, None, None),
    )
    return jax.shard_map(
        local,
        mesh=split,
        in_specs=placed,
        out_specs=(P(grp, None, "se"), P(None, every)),
        check_vma=False,
    )
```

```python
import jax
import jax.numpy as jnp
from jax import lax
from jax.experimental import pallas as pl
from jax.experimental.pallas import tpu as pltpu
from jax.sharding import PartitionSpec as P

ROOT = 4096
CAPACITY = 2
RC = 16
LANES = 128
EARLY = 3840
EMPTY = 64.0
BF16 = jnp.bfloat16
F32 = jnp.float32
I32 = jnp.int32
VMEM = pl.BlockSpec(memory_space=pltpu.VMEM)
SMEM = pl.BlockSpec(memory_space=pltpu.SMEM)
ANY = pl.BlockSpec(memory_space=pl.ANY)
WIDE = pltpu.CompilerParams(vmem_limit_bytes=62 * 1024 * 1024)
ROOMY = pltpu.CompilerParams(vmem_limit_bytes=50 * 1024 * 1024)
LIMIT = pltpu.CompilerParams(vmem_limit_bytes=16 * 1024 * 1024)


def iota(shape, dim):
    return lax.broadcasted_iota(I32, shape, dim)


def dot_nt(a, b):
    return lax.dot_general(a, b, (((1,), (1,)), ((), ())), preferred_element_type=F32)


def dot_tn(a, b):
    return lax.dot_general(a, b, (((0,), (0,)), ((), ())), preferred_element_type=F32)


def one_hot(hits):
    return hits.astype(F32).astype(BF16)


def pack_kernel(owner_ref, pressure_ref, out_ref, held_ref, owner_smem, count_ref, owner_sem, block_sem):
    slots = out_ref.shape[0]
    owners = pltpu.make_async_copy(owner_ref, owner_smem, owner_sem)
    blocks = pltpu.make_async_copy(pressure_ref, held_ref, block_sem)
    owners.start()
    blocks.start()
    out_ref[:, 0:16, :] = jnp.full((slots, 16, out_ref.shape[2]), EMPTY, BF16)
    for e in range(slots // CAPACITY):
        count_ref[e] = 0
    owners.wait()
    blocks.wait()
    for t in range(held_ref.shape[0]):
        owner = owner_smem[t]
        count = count_ref[owner]
        count_ref[owner] = count + 1
        out_ref[owner * CAPACITY + count] = held_ref[t]


def pack(block_owner, pressure, members):
    blocks, cases, rows = pressure.shape
    return pl.pallas_call(
        pack_kernel,
        out_shape=jax.ShapeDtypeStruct((members * CAPACITY, cases, rows), BF16),
        in_specs=[ANY, ANY],
        out_specs=VMEM,
        scratch_shapes=[
            pltpu.VMEM((blocks, cases, rows), BF16),
            pltpu.SMEM((blocks,), I32),
            pltpu.SMEM((members,), I32),
            pltpu.SemaphoreType.DMA,
            pltpu.SemaphoreType.DMA,
        ],
        compiler_params=WIDE,
    )(block_owner, pressure)


def bring_kernel(level_ref, out_ref, sem):
    copy = pltpu.make_async_copy(level_ref.at[:, 0 : out_ref.shape[1]], out_ref, sem)
    copy.start()
    copy.wait()


def bring(matrix):
    return pl.pallas_call(
        bring_kernel,
        out_shape=jax.ShapeDtypeStruct((matrix.shape[0], EARLY), BF16),
        in_specs=[ANY],
        out_specs=VMEM,
        scratch_shapes=[pltpu.SemaphoreType.DMA],
        compiler_params=pltpu.CompilerParams(vmem_limit_bytes=48 * 1024 * 1024),
    )(matrix)


def condense_kernel(
    incoming_ref, early_ref, level_ref, slot_ref, target_ref, out_ref, late_ref, interior_ref, level_sem
):
    slots, cases, rows = incoming_ref.shape
    depth = level_ref.shape[1]
    most = depth // rows
    late = pltpu.make_async_copy(level_ref.at[:, EARLY:depth], late_ref, level_sem)
    late.start()
    interior_ref[...] = jnp.zeros_like(interior_ref)
    marks = incoming_ref[:, 0:16, :].astype(F32)[:, 0, 0:1]
    filled = (marks < EMPTY / 2).astype(F32)
    row, col = iota((slots, LANES), 0), iota((slots, LANES), 1)
    before = jnp.sum(jnp.where(row < col, filled, 0.0), axis=0, keepdims=True)
    here = jnp.sum(jnp.where(row == col, filled, 0.0), axis=0, keepdims=True)
    place = jnp.where(here > 0.5, before, float(most)).astype(I32) * rows
    for q in range(slots):
        at = pl.multiple_of(place[0, q], rows)
        interior_ref[0:cases, pl.ds(at, rows)] = incoming_ref[q]
    boundary = dot_nt(early_ref[...], interior_ref[:, 0:EARLY])
    late.wait()
    boundary += dot_nt(late_ref[...], interior_ref[:, EARLY:depth])
    parts = cases // 2
    lane = iota(boundary.shape, 1)
    dest = target_ref[...] // rows
    offset = (target_ref[...] - dest * rows + 1).astype(F32)
    own = jnp.where(lane == cases + parts, offset, jnp.where(lane < cases, boundary, 0.0))
    lower = pltpu.roll(boundary, cases, 1)
    upper = pltpu.roll(boundary, parts, 1)
    other = jnp.where(dest % 2 == 1, lower, upper)
    other = jnp.where((lane >= cases) & (lane < cases + parts), other, 0.0)
    other = jnp.where(lane == cases + parts + 1, offset, other)
    slot = slot_ref[...]
    want = iota((out_ref.shape[0], slot.shape[1]), 0)
    sent = jnp.dot(one_hot(slot == want), own.astype(BF16), preferred_element_type=F32)
    sent += jnp.dot(one_hot(slot == want ^ RC), other.astype(BF16), preferred_element_type=F32)
    out_ref[...] = sent.astype(BF16)


def condense(incoming, early, matrix, slot, target, members):
    depth = matrix.shape[1]
    rows = incoming.shape[2]
    return pl.pallas_call(
        condense_kernel,
        out_shape=jax.ShapeDtypeStruct((members * RC, LANES), BF16),
        in_specs=[VMEM, VMEM, ANY, VMEM, VMEM],
        out_specs=VMEM,
        scratch_shapes=[
            pltpu.VMEM((matrix.shape[0], depth - EARLY), BF16),
            pltpu.VMEM((LANES, depth + rows), BF16),
            pltpu.SemaphoreType.DMA,
        ],
        compiler_params=ROOMY,
    )(incoming, early, matrix, slot, target)


def assemble_kernel(side_ref, rows_ref, matrix_ref, other_ref, load_ref, out_ref):
    cases = load_ref.shape[0]
    parts = cases // 2
    rows = rows_ref[...]
    offsets = rows.astype(F32)[:, cases + parts : cases + parts + 2]
    want = (iota(rows.shape, 1) + 1).astype(F32)
    load = dot_tn(rows, one_hot(offsets[:, 0:1] == want))[0:cases]
    other = dot_tn(rows, one_hot(offsets[:, 1:2] == want))[cases : cases + parts]
    load_ref[...] = load
    second = dot_nt(load.astype(BF16), matrix_ref[...])
    second = jnp.where(side_ref[0] == 0, second[0:parts], second[parts:cases])
    out_ref[...] = (second + dot_nt(other.astype(BF16), other_ref[...])).astype(BF16)


def assemble(side, rows, matrix, other, cases):
    half = matrix.shape[1]
    return pl.pallas_call(
        assemble_kernel,
        out_shape=(
            jax.ShapeDtypeStruct((cases, half), F32),
            jax.ShapeDtypeStruct((cases // 2, LANES), BF16),
        ),
        in_specs=[SMEM, VMEM, VMEM, VMEM],
        out_specs=(VMEM, VMEM),
        compiler_params=LIMIT,
    )(side, rows, matrix, other)


def root_kernel(key_ref, mine_ref, theirs_ref, out_ref):
    rows = out_ref.shape[0]
    parts = mine_ref.shape[0]
    share = LANES // parts
    row = iota((rows, LANES), 0)
    both = jnp.concatenate([mine_ref[...], theirs_ref[...]], axis=1)
    zero = jnp.zeros_like(both)
    total = jnp.zeros(out_ref.shape, F32)
    for k in range(share):
        hits = [one_hot(row * share + k == key_ref[c : c + 1, :]) for c in range(2)]
        placed = jnp.concatenate([both if j == k else zero for j in range(share)], axis=0)
        total += dot_nt(jnp.concatenate(hits, axis=1), placed)
    out_ref[...] = total.astype(BF16)


def root_sum(key, mine, theirs, rows):
    return pl.pallas_call(
        root_kernel,
        out_shape=jax.ShapeDtypeStruct((rows, LANES), BF16),
        in_specs=[VMEM, VMEM, VMEM],
        out_specs=VMEM,
        compiler_params=LIMIT,
    )(key, mine, theirs)


def last_kernel(shares_ref, out_ref):
    columns, cases = out_ref.shape
    parts = cases // 2
    share = LANES // parts
    each = columns // share
    period = 2 * each
    total = jnp.zeros((16, LANES), F32)
    for s in range(shares_ref.shape[0] // 16):
        total += shares_ref[16 * s : 16 * s + 16, :].astype(F32)
    halves = total[0:period]
    for s in range(1, 16 // period):
        halves += total[s * period : (s + 1) * period]
    for k in range(share):
        lanes = halves[:, k * parts : (k + 1) * parts]
        both = jnp.concatenate([lanes[0:each], lanes[each:period]], axis=1)
        for i in range(each):
            out_ref[i * share + k : i * share + k + 1, :] = both[i : i + 1]


def last_sum(shares, columns, cases):
    return pl.pallas_call(
        last_kernel,
        out_shape=jax.ShapeDtypeStruct((columns, cases), F32),
        in_specs=[VMEM],
        out_specs=VMEM,
        compiler_params=LIMIT,
    )(shares)


def exchange(x, axis):
    return lax.all_to_all(x, axis, split_axis=0, concat_axis=0, tiled=True)


def local(pressure, block_owner, level_one, level_one_map, level_two, level_two_map):
    members = lax.axis_size("se")
    groups = lax.axis_size("y") * lax.axis_size("core")
    core = lax.axis_index("core")
    member = lax.axis_index("se")
    cases = pressure.shape[1]
    half = level_two.shape[2]

    outgoing = pack(block_owner, pressure, members)
    incoming = exchange(outgoing, "se")

    target = level_one_map[0]
    early = bring(level_one[0])
    dest = target // half
    dofs = jnp.arange(target.shape[0], dtype=I32)
    earlier = (dest[:, None] == dest[None, :]) & (dofs[:, None] < dofs[None, :])
    slot = dest * RC + jnp.sum(earlier.astype(I32), axis=0)
    root = lax.dynamic_index_in_dim(level_two_map[0], member // 2, 0, keepdims=True)
    side = (member % 2)[None]
    partner = lax.ppermute(level_two[0], "se", [(i, i ^ 1) for i in range(members)])
    span = ROOT // groups
    roots = jnp.concatenate([root, lax.ppermute(root, "core", [(0, 1), (1, 0)])], axis=0)
    group = roots // span
    key = jnp.where(group % 2 == core, group // 2 * span + roots % span, -1)
    target, partner, key, early = lax.optimization_barrier((target, partner, key, early))

    packed = condense(incoming, early, level_one[0], slot[None, :], target[:, None], members)
    received = exchange(packed.reshape(members, RC, LANES), "se").reshape(members * RC, LANES)
    level_two_load, second = assemble(side, received, level_two[0], partner, cases)
    theirs = lax.ppermute(second, "core", [(0, 1), (1, 0)])
    columns = span // members
    share = root_sum(key, second, theirs, groups // 2 * span * (cases // 2) // LANES)
    share = exchange(share, ("y", "se"))
    root_load = last_sum(share, columns, cases).T
    return (level_two_load[None], root_load)


def solution(mesh):
    groups, members = mesh.devices.shape
    split = jax.sharding.Mesh(mesh.devices.reshape(groups // 2, 2, members), ("y", "core", "se"))
    grp = ("y", "core")
    every = ("y", "core", "se")
    placed = (
        P(every, None, None),
        P(every),
        P(every, None, None),
        P(every, None),
        P(grp, None, "se"),
        P(grp, None, None),
    )
    return jax.shard_map(
        local,
        mesh=split,
        in_specs=placed,
        out_specs=(P(grp, None, "se"), P(None, every)),
        check_vma=False,
    )
```

```python
import jax
import jax.numpy as jnp
from jax import lax
from jax.experimental import pallas as pl
from jax.experimental.pallas import tpu as pltpu
from jax.sharding import PartitionSpec as P

ROOT = 4096
CAPACITY = 2
RC = 16
LANES = 128
EARLY = 3840
EMPTY = 64.0
BF16 = jnp.bfloat16
F32 = jnp.float32
I32 = jnp.int32
VMEM = pl.BlockSpec(memory_space=pltpu.VMEM)
SMEM = pl.BlockSpec(memory_space=pltpu.SMEM)
ANY = pl.BlockSpec(memory_space=pl.ANY)
WIDE = pltpu.CompilerParams(vmem_limit_bytes=62 * 1024 * 1024)
ROOMY = pltpu.CompilerParams(vmem_limit_bytes=50 * 1024 * 1024)
LIMIT = pltpu.CompilerParams(vmem_limit_bytes=16 * 1024 * 1024)


def iota(shape, dim):
    return lax.broadcasted_iota(I32, shape, dim)


def dot_nt(a, b):
    return lax.dot_general(a, b, (((1,), (1,)), ((), ())), preferred_element_type=F32)


def dot_tn(a, b):
    return lax.dot_general(a, b, (((0,), (0,)), ((), ())), preferred_element_type=F32)


def one_hot(hits):
    return hits.astype(F32).astype(BF16)


def pack_kernel(owner_ref, pressure_ref, out_ref, held_ref, owner_smem, count_ref, owner_sem, block_sem):
    slots = out_ref.shape[0]
    owners = pltpu.make_async_copy(owner_ref, owner_smem, owner_sem)
    blocks = pltpu.make_async_copy(pressure_ref, held_ref, block_sem)
    owners.start()
    blocks.start()
    out_ref[:, 0:16, :] = jnp.full((slots, 16, out_ref.shape[2]), EMPTY, BF16)
    for e in range(slots // CAPACITY):
        count_ref[e] = 0
    owners.wait()
    blocks.wait()
    for t in range(held_ref.shape[0]):
        owner = owner_smem[t]
        count = count_ref[owner]
        count_ref[owner] = count + 1
        out_ref[owner * CAPACITY + count] = held_ref[t]


def pack(block_owner, pressure, members):
    blocks, cases, rows = pressure.shape
    return pl.pallas_call(
        pack_kernel,
        out_shape=jax.ShapeDtypeStruct((members * CAPACITY, cases, rows), BF16),
        in_specs=[ANY, ANY],
        out_specs=VMEM,
        scratch_shapes=[
            pltpu.VMEM((blocks, cases, rows), BF16),
            pltpu.SMEM((blocks,), I32),
            pltpu.SMEM((members,), I32),
            pltpu.SemaphoreType.DMA,
            pltpu.SemaphoreType.DMA,
        ],
        compiler_params=WIDE,
    )(block_owner, pressure)


def bring_kernel(level_ref, out_ref, sem):
    copy = pltpu.make_async_copy(level_ref.at[:, 0 : out_ref.shape[1]], out_ref, sem)
    copy.start()
    copy.wait()


def bring(matrix):
    return pl.pallas_call(
        bring_kernel,
        out_shape=jax.ShapeDtypeStruct((matrix.shape[0], EARLY), BF16),
        in_specs=[ANY],
        out_specs=VMEM,
        scratch_shapes=[pltpu.SemaphoreType.DMA],
        compiler_params=pltpu.CompilerParams(vmem_limit_bytes=48 * 1024 * 1024),
    )(matrix)


def condense_kernel(
    incoming_ref, early_ref, level_ref, slot_ref, target_ref, out_ref, late_ref, interior_ref, level_sem
):
    slots, cases, rows = incoming_ref.shape
    depth = level_ref.shape[1]
    most = depth // rows
    late = pltpu.make_async_copy(level_ref.at[:, EARLY:depth], late_ref, level_sem)
    late.start()
    interior_ref[...] = jnp.zeros_like(interior_ref)
    marks = incoming_ref[:, 0:16, :].astype(F32)[:, 0, 0:1]
    filled = (marks < EMPTY / 2).astype(F32)
    row, col = iota((slots, LANES), 0), iota((slots, LANES), 1)
    before = jnp.sum(jnp.where(row < col, filled, 0.0), axis=0, keepdims=True)
    here = jnp.sum(jnp.where(row == col, filled, 0.0), axis=0, keepdims=True)
    place = jnp.where(here > 0.5, before, float(most)).astype(I32) * rows
    for q in range(slots):
        at = pl.multiple_of(place[0, q], rows)
        interior_ref[0:cases, pl.ds(at, rows)] = incoming_ref[q]
    boundary = dot_nt(early_ref[...], interior_ref[:, 0:EARLY])
    late.wait()
    boundary += dot_nt(late_ref[...], interior_ref[:, EARLY:depth])
    parts = cases // 2
    lane = iota(boundary.shape, 1)
    dest = target_ref[...] // rows
    offset = (target_ref[...] - dest * rows + 1).astype(F32)
    own = jnp.where(lane == cases + parts, offset, jnp.where(lane < cases, boundary, 0.0))
    lower = pltpu.roll(boundary, cases, 1)
    upper = pltpu.roll(boundary, parts, 1)
    other = jnp.where(dest % 2 == 1, lower, upper)
    other = jnp.where((lane >= cases) & (lane < cases + parts), other, 0.0)
    other = jnp.where(lane == cases + parts + 1, offset, other)
    slot = slot_ref[...]
    want = iota((out_ref.shape[0], slot.shape[1]), 0)
    sent = jnp.dot(one_hot(slot == want), own.astype(BF16), preferred_element_type=F32)
    sent += jnp.dot(one_hot(slot == want ^ RC), other.astype(BF16), preferred_element_type=F32)
    out_ref[...] = sent.astype(BF16)


def condense(incoming, early, matrix, slot, target, members):
    depth = matrix.shape[1]
    rows = incoming.shape[2]
    return pl.pallas_call(
        condense_kernel,
        out_shape=jax.ShapeDtypeStruct((members * RC, LANES), BF16),
        in_specs=[VMEM, VMEM, ANY, VMEM, VMEM],
        out_specs=VMEM,
        scratch_shapes=[
            pltpu.VMEM((matrix.shape[0], depth - EARLY), BF16),
            pltpu.VMEM((LANES, depth + rows), BF16),
            pltpu.SemaphoreType.DMA,
        ],
        compiler_params=ROOMY,
    )(incoming, early, matrix, slot, target)


def assemble_kernel(side_ref, rows_ref, matrix_ref, other_ref, load_ref, out_ref):
    cases = load_ref.shape[0]
    parts = cases // 2
    rows = rows_ref[...]
    offsets = rows.astype(F32)[:, cases + parts : cases + parts + 2]
    want = (iota(rows.shape, 1) + 1).astype(F32)
    load = dot_tn(rows, one_hot(offsets[:, 0:1] == want))[0:cases]
    other = dot_tn(rows, one_hot(offsets[:, 1:2] == want))[cases : cases + parts]
    load_ref[...] = load
    second = dot_nt(load.astype(BF16), matrix_ref[...])
    second = jnp.where(side_ref[0] == 0, second[0:parts], second[parts:cases])
    out_ref[...] = (second + dot_nt(other.astype(BF16), other_ref[...])).astype(BF16)


def assemble(side, rows, matrix, other, cases):
    half = matrix.shape[1]
    return pl.pallas_call(
        assemble_kernel,
        out_shape=(
            jax.ShapeDtypeStruct((cases, half), F32),
            jax.ShapeDtypeStruct((cases // 2, LANES), BF16),
        ),
        in_specs=[SMEM, VMEM, VMEM, VMEM],
        out_specs=(VMEM, VMEM),
        compiler_params=LIMIT,
    )(side, rows, matrix, other)


def root_kernel(key_ref, mine_ref, theirs_ref, out_ref):
    rows = out_ref.shape[0]
    parts = mine_ref.shape[0]
    share = LANES // parts
    row = iota((rows, LANES), 0)
    both = jnp.concatenate([mine_ref[...], theirs_ref[...]], axis=1)
    zero = jnp.zeros_like(both)
    total = jnp.zeros(out_ref.shape, F32)
    for k in range(share):
        hits = [one_hot(row * share + k == key_ref[c : c + 1, :]) for c in range(2)]
        placed = jnp.concatenate([both if j == k else zero for j in range(share)], axis=0)
        total += dot_nt(jnp.concatenate(hits, axis=1), placed)
    out_ref[...] = total.astype(BF16)


def root_sum(key, mine, theirs, rows):
    return pl.pallas_call(
        root_kernel,
        out_shape=jax.ShapeDtypeStruct((rows, LANES), BF16),
        in_specs=[VMEM, VMEM, VMEM],
        out_specs=VMEM,
        compiler_params=LIMIT,
    )(key, mine, theirs)


def last_kernel(shares_ref, out_ref):
    columns, cases = out_ref.shape
    parts = cases // 2
    share = LANES // parts
    each = columns // share
    period = 2 * each
    total = jnp.zeros((16, LANES), F32)
    for s in range(shares_ref.shape[0] // 16):
        total += shares_ref[16 * s : 16 * s + 16, :].astype(F32)
    halves = total[0:period]
    for s in range(1, 16 // period):
        halves += total[s * period : (s + 1) * period]
    for k in range(share):
        lanes = halves[:, k * parts : (k + 1) * parts]
        both = jnp.concatenate([lanes[0:each], lanes[each:period]], axis=1)
        for i in range(each):
            out_ref[i * share + k : i * share + k + 1, :] = both[i : i + 1]


def last_sum(shares, columns, cases):
    return pl.pallas_call(
        last_kernel,
        out_shape=jax.ShapeDtypeStruct((columns, cases), F32),
        in_specs=[VMEM],
        out_specs=VMEM,
        compiler_params=LIMIT,
    )(shares)


def exchange(x, axis):
    return lax.all_to_all(x, axis, split_axis=0, concat_axis=0, tiled=True)


def local(pressure, block_owner, level_one, level_one_map, level_two, level_two_map):
    members = lax.axis_size("se")
    groups = lax.axis_size("y") * lax.axis_size("core")
    core = lax.axis_index("core")
    member = lax.axis_index("se")
    cases = pressure.shape[1]
    half = level_two.shape[2]

    outgoing = pack(block_owner, pressure, members)
    incoming = exchange(outgoing, "se")

    target = level_one_map[0]
    early = bring(level_one[0])
    dest = target // half
    dofs = jnp.arange(target.shape[0], dtype=I32)
    earlier = (dest[:, None] == dest[None, :]) & (dofs[:, None] < dofs[None, :])
    slot = dest * RC + jnp.sum(earlier.astype(I32), axis=0)
    root = lax.dynamic_index_in_dim(level_two_map[0], member // 2, 0, keepdims=True)
    side = (member % 2)[None]
    partner = lax.ppermute(level_two[0], "se", [(i, i ^ 1) for i in range(members)])
    span = ROOT // groups
    roots = jnp.concatenate([root, lax.ppermute(root, "core", [(0, 1), (1, 0)])], axis=0)
    group = roots // span
    key = jnp.where(group % 2 == core, group // 2 * span + roots % span, -1)
    target, partner, key, side, early = lax.optimization_barrier((target, partner, key, side, early))

    packed = condense(incoming, early, level_one[0], slot[None, :], target[:, None], members)
    received = exchange(packed.reshape(members, RC, LANES), "se").reshape(members * RC, LANES)
    level_two_load, second = assemble(side, received, level_two[0], partner, cases)
    theirs = lax.ppermute(second, "core", [(0, 1), (1, 0)])
    columns = span // members
    share = root_sum(key, second, theirs, groups // 2 * span * (cases // 2) // LANES)
    share = exchange(share, ("y", "se"))
    root_load = last_sum(share, columns, cases).T
    return (level_two_load[None], root_load)


def solution(mesh):
    groups, members = mesh.devices.shape
    split = jax.sharding.Mesh(mesh.devices.reshape(groups // 2, 2, members), ("y", "core", "se"))
    grp = ("y", "core")
    every = ("y", "core", "se")
    placed = (
        P(every, None, None),
        P(every),
        P(every, None, None),
        P(every, None),
        P(grp, None, "se"),
        P(grp, None, None),
    )
    return jax.shard_map(
        local,
        mesh=split,
        in_specs=placed,
        out_specs=(P(grp, None, "se"), P(None, every)),
        check_vma=False,
    )
```

```python
import jax
import jax.numpy as jnp
from jax import lax
from jax.experimental import pallas as pl
from jax.experimental.pallas import tpu as pltpu
from jax.sharding import PartitionSpec as P

ROOT = 4096
CAPACITY = 2
RC = 16
LANES = 128
EARLY = 3072
EMPTY = 64.0
BF16 = jnp.bfloat16
F32 = jnp.float32
I32 = jnp.int32
VMEM = pl.BlockSpec(memory_space=pltpu.VMEM)
SMEM = pl.BlockSpec(memory_space=pltpu.SMEM)
ANY = pl.BlockSpec(memory_space=pl.ANY)
WIDE = pltpu.CompilerParams(vmem_limit_bytes=62 * 1024 * 1024)
ROOMY = pltpu.CompilerParams(vmem_limit_bytes=50 * 1024 * 1024)
LIMIT = pltpu.CompilerParams(vmem_limit_bytes=16 * 1024 * 1024)


def iota(shape, dim):
    return lax.broadcasted_iota(I32, shape, dim)


def dot_nt(a, b):
    return lax.dot_general(a, b, (((1,), (1,)), ((), ())), preferred_element_type=F32)


def dot_tn(a, b):
    return lax.dot_general(a, b, (((0,), (0,)), ((), ())), preferred_element_type=F32)


def one_hot(hits):
    return hits.astype(F32).astype(BF16)


def pack_kernel(owner_ref, pressure_ref, out_ref, held_ref, owner_smem, count_ref, owner_sem, block_sem):
    slots = out_ref.shape[0]
    owners = pltpu.make_async_copy(owner_ref, owner_smem, owner_sem)
    blocks = pltpu.make_async_copy(pressure_ref, held_ref, block_sem)
    owners.start()
    blocks.start()
    out_ref[:, 0:16, :] = jnp.full((slots, 16, out_ref.shape[2]), EMPTY, BF16)
    for e in range(slots // CAPACITY):
        count_ref[e] = 0
    owners.wait()
    blocks.wait()
    for t in range(held_ref.shape[0]):
        owner = owner_smem[t]
        count = count_ref[owner]
        count_ref[owner] = count + 1
        out_ref[owner * CAPACITY + count] = held_ref[t]


def pack(block_owner, pressure, members):
    blocks, cases, rows = pressure.shape
    return pl.pallas_call(
        pack_kernel,
        out_shape=jax.ShapeDtypeStruct((members * CAPACITY, cases, rows), BF16),
        in_specs=[ANY, ANY],
        out_specs=VMEM,
        scratch_shapes=[
            pltpu.VMEM((blocks, cases, rows), BF16),
            pltpu.SMEM((blocks,), I32),
            pltpu.SMEM((members,), I32),
            pltpu.SemaphoreType.DMA,
            pltpu.SemaphoreType.DMA,
        ],
        compiler_params=WIDE,
    )(block_owner, pressure)


def bring_kernel(level_ref, out_ref, sem):
    copy = pltpu.make_async_copy(level_ref.at[:, 0 : out_ref.shape[1]], out_ref, sem)
    copy.start()
    copy.wait()


def bring(matrix):
    return pl.pallas_call(
        bring_kernel,
        out_shape=jax.ShapeDtypeStruct((matrix.shape[0], EARLY), BF16),
        in_specs=[ANY],
        out_specs=VMEM,
        scratch_shapes=[pltpu.SemaphoreType.DMA],
        compiler_params=pltpu.CompilerParams(vmem_limit_bytes=48 * 1024 * 1024),
    )(matrix)


def condense_kernel(
    incoming_ref, early_ref, level_ref, slot_ref, target_ref, out_ref, late_ref, interior_ref, level_sem
):
    slots, cases, rows = incoming_ref.shape
    depth = level_ref.shape[1]
    most = depth // rows
    late = pltpu.make_async_copy(level_ref.at[:, EARLY:depth], late_ref, level_sem)
    late.start()
    interior_ref[...] = jnp.zeros_like(interior_ref)
    marks = incoming_ref[:, 0:16, :].astype(F32)[:, 0, 0:1]
    filled = (marks < EMPTY / 2).astype(F32)
    row, col = iota((slots, LANES), 0), iota((slots, LANES), 1)
    before = jnp.sum(jnp.where(row < col, filled, 0.0), axis=0, keepdims=True)
    here = jnp.sum(jnp.where(row == col, filled, 0.0), axis=0, keepdims=True)
    place = jnp.where(here > 0.5, before, float(most)).astype(I32) * rows
    for q in range(slots):
        at = pl.multiple_of(place[0, q], rows)
        interior_ref[0:cases, pl.ds(at, rows)] = incoming_ref[q]
    boundary = dot_nt(early_ref[...], interior_ref[:, 0:EARLY])
    late.wait()
    boundary += dot_nt(late_ref[...], interior_ref[:, EARLY:depth])
    parts = cases // 2
    lane = iota(boundary.shape, 1)
    dest = target_ref[...] // rows
    offset = (target_ref[...] - dest * rows + 1).astype(F32)
    own = jnp.where(lane == cases + parts, offset, jnp.where(lane < cases, boundary, 0.0))
    lower = pltpu.roll(boundary, cases, 1)
    upper = pltpu.roll(boundary, parts, 1)
    other = jnp.where(dest % 2 == 1, lower, upper)
    other = jnp.where((lane >= cases) & (lane < cases + parts), other, 0.0)
    other = jnp.where(lane == cases + parts + 1, offset, other)
    slot = slot_ref[...]
    choose = one_hot(slot == iota((out_ref.shape[0], slot.shape[1]), 0))
    both = jnp.concatenate([own, other], axis=1).astype(BF16)
    chosen = jnp.dot(choose, both, preferred_element_type=F32)
    blocks = chosen[:, LANES : 2 * LANES].reshape(-1, 2, RC, LANES)
    swapped = jnp.concatenate([blocks[:, 1:2], blocks[:, 0:1]], axis=1)
    sent = chosen[:, 0:LANES] + swapped.reshape(-1, LANES)
    out_ref[...] = sent.astype(BF16)


def condense(incoming, early, matrix, slot, target, members):
    depth = matrix.shape[1]
    rows = incoming.shape[2]
    return pl.pallas_call(
        condense_kernel,
        out_shape=jax.ShapeDtypeStruct((members * RC, LANES), BF16),
        in_specs=[VMEM, VMEM, ANY, VMEM, VMEM],
        out_specs=VMEM,
        scratch_shapes=[
            pltpu.VMEM((matrix.shape[0], depth - EARLY), BF16),
            pltpu.VMEM((LANES, depth + rows), BF16),
            pltpu.SemaphoreType.DMA,
        ],
        compiler_params=ROOMY,
    )(incoming, early, matrix, slot, target)


def assemble_kernel(side_ref, rows_ref, matrix_ref, other_ref, load_ref, out_ref):
    cases = load_ref.shape[0]
    parts = cases // 2
    rows = rows_ref[...]
    offsets = rows.astype(F32)[:, cases + parts : cases + parts + 2]
    want = (iota(rows.shape, 1) + 1).astype(F32)
    hits = jnp.concatenate([one_hot(offsets[:, 0:1] == want), one_hot(offsets[:, 1:2] == want)], axis=1)
    loads = dot_tn(rows, hits)
    load = loads[0:cases, 0:LANES]
    other = loads[cases : cases + parts, LANES : 2 * LANES]
    load_ref[...] = load
    second = dot_nt(load.astype(BF16), matrix_ref[...])
    second = jnp.where(side_ref[0] == 0, second[0:parts], second[parts:cases])
    out_ref[...] = (second + dot_nt(other.astype(BF16), other_ref[...])).astype(BF16)


def assemble(side, rows, matrix, other, cases):
    half = matrix.shape[1]
    return pl.pallas_call(
        assemble_kernel,
        out_shape=(
            jax.ShapeDtypeStruct((cases, half), F32),
            jax.ShapeDtypeStruct((cases // 2, LANES), BF16),
        ),
        in_specs=[SMEM, VMEM, VMEM, VMEM],
        out_specs=(VMEM, VMEM),
        compiler_params=LIMIT,
    )(side, rows, matrix, other)


def root_kernel(key_ref, mine_ref, theirs_ref, out_ref):
    rows = out_ref.shape[0]
    parts = mine_ref.shape[0]
    share = LANES // parts
    row = iota((rows, LANES), 0)
    both = jnp.concatenate([mine_ref[...], theirs_ref[...]], axis=1)
    zero = jnp.zeros_like(both)
    total = jnp.zeros(out_ref.shape, F32)
    for k in range(share):
        hits = [one_hot(row * share + k == key_ref[c : c + 1, :]) for c in range(2)]
        placed = jnp.concatenate([both if j == k else zero for j in range(share)], axis=0)
        total += dot_nt(jnp.concatenate(hits, axis=1), placed)
    out_ref[...] = total.astype(BF16)


def root_sum(key, mine, theirs, rows):
    return pl.pallas_call(
        root_kernel,
        out_shape=jax.ShapeDtypeStruct((rows, LANES), BF16),
        in_specs=[VMEM, VMEM, VMEM],
        out_specs=VMEM,
        compiler_params=LIMIT,
    )(key, mine, theirs)


def last_kernel(shares_ref, out_ref):
    columns, cases = out_ref.shape
    parts = cases // 2
    share = LANES // parts
    each = columns // share
    period = 2 * each
    total = jnp.zeros((16, LANES), F32)
    for s in range(shares_ref.shape[0] // 16):
        total += shares_ref[16 * s : 16 * s + 16, :].astype(F32)
    halves = total[0:period]
    for s in range(1, 16 // period):
        halves += total[s * period : (s + 1) * period]
    for k in range(share):
        lanes = halves[:, k * parts : (k + 1) * parts]
        both = jnp.concatenate([lanes[0:each], lanes[each:period]], axis=1)
        for i in range(each):
            out_ref[i * share + k : i * share + k + 1, :] = both[i : i + 1]


def last_sum(shares, columns, cases):
    return pl.pallas_call(
        last_kernel,
        out_shape=jax.ShapeDtypeStruct((columns, cases), F32),
        in_specs=[VMEM],
        out_specs=VMEM,
        compiler_params=LIMIT,
    )(shares)


def exchange(x, axis):
    return lax.all_to_all(x, axis, split_axis=0, concat_axis=0, tiled=True)


def local(pressure, block_owner, level_one, level_one_map, level_two, level_two_map):
    members = lax.axis_size("se")
    groups = lax.axis_size("y") * lax.axis_size("core")
    core = lax.axis_index("core")
    member = lax.axis_index("se")
    cases = pressure.shape[1]
    half = level_two.shape[2]

    outgoing = pack(block_owner, pressure, members)
    incoming = exchange(outgoing, "se")

    target = level_one_map[0]
    early = bring(level_one[0])
    dest = target // half
    dofs = jnp.arange(target.shape[0], dtype=I32)
    earlier = (dest[:, None] == dest[None, :]) & (dofs[:, None] < dofs[None, :])
    slot = dest * RC + jnp.sum(earlier.astype(I32), axis=0)
    root = lax.dynamic_index_in_dim(level_two_map[0], member // 2, 0, keepdims=True)
    side = (member % 2)[None]
    partner = lax.ppermute(level_two[0], "se", [(i, i ^ 1) for i in range(members)])
    span = ROOT // groups
    roots = jnp.concatenate([root, lax.ppermute(root, "core", [(0, 1), (1, 0)])], axis=0)
    group = roots // span
    key = jnp.where(group % 2 == core, group // 2 * span + roots % span, -1)
    target, partner, key, side, early = lax.optimization_barrier((target, partner, key, side, early))

    packed = condense(incoming, early, level_one[0], slot[None, :], target[:, None], members)
    received = exchange(packed.reshape(members, RC, LANES), "se").reshape(members * RC, LANES)
    level_two_load, second = assemble(side, received, level_two[0], partner, cases)
    theirs = lax.ppermute(second, "core", [(0, 1), (1, 0)])
    columns = span // members
    share = root_sum(key, second, theirs, groups // 2 * span * (cases // 2) // LANES)
    share = exchange(share, ("y", "se"))
    root_load = last_sum(share, columns, cases).T
    return (level_two_load[None], root_load)


def solution(mesh):
    groups, members = mesh.devices.shape
    split = jax.sharding.Mesh(mesh.devices.reshape(groups // 2, 2, members), ("y", "core", "se"))
    grp = ("y", "core")
    every = ("y", "core", "se")
    placed = (
        P(every, None, None),
        P(every),
        P(every, None, None),
        P(every, None),
        P(grp, None, "se"),
        P(grp, None, None),
    )
    return jax.shard_map(
        local,
        mesh=split,
        in_specs=placed,
        out_specs=(P(grp, None, "se"), P(None, every)),
        check_vma=False,
    )
```

```python
import jax
import jax.numpy as jnp
from jax import lax
from jax.experimental import pallas as pl
from jax.experimental.pallas import tpu as pltpu
from jax.sharding import PartitionSpec as P

ROOT = 4096
CAPACITY = 2
RC = 16
LANES = 128
EARLY = 3072
EMPTY = 64.0
BF16 = jnp.bfloat16
F32 = jnp.float32
I32 = jnp.int32
VMEM = pl.BlockSpec(memory_space=pltpu.VMEM)
SMEM = pl.BlockSpec(memory_space=pltpu.SMEM)
ANY = pl.BlockSpec(memory_space=pl.ANY)
WIDE = pltpu.CompilerParams(vmem_limit_bytes=62 * 1024 * 1024)
ROOMY = pltpu.CompilerParams(vmem_limit_bytes=50 * 1024 * 1024)
LIMIT = pltpu.CompilerParams(vmem_limit_bytes=16 * 1024 * 1024)


def iota(shape, dim):
    return lax.broadcasted_iota(I32, shape, dim)


def dot_nt(a, b):
    return lax.dot_general(a, b, (((1,), (1,)), ((), ())), preferred_element_type=F32)


def dot_tn(a, b):
    return lax.dot_general(a, b, (((0,), (0,)), ((), ())), preferred_element_type=F32)


def one_hot(hits):
    return hits.astype(F32).astype(BF16)


def pack_kernel(owner_ref, pressure_ref, out_ref, held_ref, owner_smem, count_ref, owner_sem, block_sem):
    slots = out_ref.shape[0]
    owners = pltpu.make_async_copy(owner_ref, owner_smem, owner_sem)
    blocks = pltpu.make_async_copy(pressure_ref, held_ref, block_sem)
    owners.start()
    blocks.start()
    out_ref[:, 0:16, :] = jnp.full((slots, 16, out_ref.shape[2]), EMPTY, BF16)
    for e in range(slots // CAPACITY):
        count_ref[e] = 0
    owners.wait()
    blocks.wait()
    for t in range(held_ref.shape[0]):
        owner = owner_smem[t]
        count = count_ref[owner]
        count_ref[owner] = count + 1
        out_ref[owner * CAPACITY + count] = held_ref[t]


def pack(block_owner, pressure, members):
    blocks, cases, rows = pressure.shape
    return pl.pallas_call(
        pack_kernel,
        out_shape=jax.ShapeDtypeStruct((members * CAPACITY, cases, rows), BF16),
        in_specs=[ANY, ANY],
        out_specs=VMEM,
        scratch_shapes=[
            pltpu.VMEM((blocks, cases, rows), BF16),
            pltpu.SMEM((blocks,), I32),
            pltpu.SMEM((members,), I32),
            pltpu.SemaphoreType.DMA,
            pltpu.SemaphoreType.DMA,
        ],
        compiler_params=WIDE,
    )(block_owner, pressure)


def bring_kernel(level_ref, out_ref, sem):
    copy = pltpu.make_async_copy(level_ref.at[:, 0 : out_ref.shape[1]], out_ref, sem)
    copy.start()
    copy.wait()


def bring(matrix):
    return pl.pallas_call(
        bring_kernel,
        out_shape=jax.ShapeDtypeStruct((matrix.shape[0], EARLY), BF16),
        in_specs=[ANY],
        out_specs=VMEM,
        scratch_shapes=[pltpu.SemaphoreType.DMA],
        compiler_params=pltpu.CompilerParams(vmem_limit_bytes=48 * 1024 * 1024),
    )(matrix)


def condense_kernel(
    incoming_ref, early_ref, level_ref, slot_ref, target_ref, out_ref, late_ref, interior_ref, level_sem
):
    slots, cases, rows = incoming_ref.shape
    depth = level_ref.shape[1]
    most = depth // rows
    late = pltpu.make_async_copy(level_ref.at[:, EARLY:depth], late_ref, level_sem)
    late.start()
    interior_ref[...] = jnp.zeros_like(interior_ref)
    marks = incoming_ref[:, 0:16, :].astype(F32)[:, 0, 0:1]
    filled = (marks < EMPTY / 2).astype(F32)
    row, col = iota((slots, LANES), 0), iota((slots, LANES), 1)
    before = jnp.sum(jnp.where(row < col, filled, 0.0), axis=0, keepdims=True)
    here = jnp.sum(jnp.where(row == col, filled, 0.0), axis=0, keepdims=True)
    place = jnp.where(here > 0.5, before, float(most)).astype(I32) * rows
    for q in range(slots):
        at = pl.multiple_of(place[0, q], rows)
        interior_ref[0:cases, pl.ds(at, rows)] = incoming_ref[q]
    boundary = dot_nt(early_ref[...], interior_ref[:, 0:EARLY])
    late.wait()
    boundary += dot_nt(late_ref[...], interior_ref[:, EARLY:depth])
    parts = cases // 2
    lane = iota(boundary.shape, 1)
    dest = target_ref[...] // rows
    offset = (target_ref[...] - dest * rows + 1).astype(F32)
    own = jnp.where(lane == cases + parts, offset, jnp.where(lane < cases, boundary, 0.0))
    lower = pltpu.roll(boundary, cases, 1)
    upper = pltpu.roll(boundary, parts, 1)
    other = jnp.where(dest % 2 == 1, lower, upper)
    other = jnp.where((lane >= cases) & (lane < cases + parts), other, 0.0)
    other = jnp.where(lane == cases + parts + 1, offset, other)
    slot = slot_ref[...]
    choose = one_hot(slot == iota((out_ref.shape[0], slot.shape[1]), 0))
    both = jnp.concatenate([own, other], axis=1).astype(BF16)
    chosen = jnp.dot(choose, both, preferred_element_type=F32)
    blocks = chosen[:, LANES : 2 * LANES].reshape(-1, 2, RC, LANES)
    swapped = jnp.concatenate([blocks[:, 1:2], blocks[:, 0:1]], axis=1)
    sent = chosen[:, 0:LANES] + swapped.reshape(-1, LANES)
    out_ref[...] = sent.astype(BF16)


def condense(incoming, early, matrix, slot, target, members):
    depth = matrix.shape[1]
    rows = incoming.shape[2]
    return pl.pallas_call(
        condense_kernel,
        out_shape=jax.ShapeDtypeStruct((members * RC, LANES), BF16),
        in_specs=[VMEM, VMEM, ANY, VMEM, VMEM],
        out_specs=VMEM,
        scratch_shapes=[
            pltpu.VMEM((matrix.shape[0], depth - EARLY), BF16),
            pltpu.VMEM((LANES, depth + rows), BF16),
            pltpu.SemaphoreType.DMA,
        ],
        compiler_params=ROOMY,
    )(incoming, early, matrix, slot, target)


def assemble_kernel(side_ref, rows_ref, matrix_ref, other_ref, load_ref, out_ref):
    cases = load_ref.shape[0]
    parts = cases // 2
    rows = rows_ref[...]
    offsets = rows.astype(F32)[:, cases + parts : cases + parts + 2]
    want = (iota(rows.shape, 1) + 1).astype(F32)
    hits = jnp.concatenate([one_hot(offsets[:, 0:1] == want), one_hot(offsets[:, 1:2] == want)], axis=1)
    loads = dot_tn(rows, hits)
    load = loads[0:cases, 0:LANES]
    other = loads[cases : cases + parts, LANES : 2 * LANES]
    load_ref[...] = load
    second = dot_nt(load.astype(BF16), matrix_ref[...])
    second = jnp.where(side_ref[0] == 0, second[0:parts], second[parts:cases])
    out_ref[...] = (second + dot_nt(other.astype(BF16), other_ref[...])).astype(BF16)


def assemble(side, rows, matrix, other, cases):
    half = matrix.shape[1]
    return pl.pallas_call(
        assemble_kernel,
        out_shape=(
            jax.ShapeDtypeStruct((cases, half), F32),
            jax.ShapeDtypeStruct((cases // 2, LANES), BF16),
        ),
        in_specs=[SMEM, VMEM, VMEM, VMEM],
        out_specs=(VMEM, VMEM),
        compiler_params=LIMIT,
    )(side, rows, matrix, other)


def root_kernel(key_ref, mine_ref, theirs_ref, out_ref):
    rows = out_ref.shape[0]
    parts = mine_ref.shape[0]
    share = LANES // parts
    row = iota((rows, LANES), 0)
    both = jnp.concatenate([mine_ref[...], theirs_ref[...]], axis=1)
    zero = jnp.zeros_like(both)
    total = jnp.zeros(out_ref.shape, F32)
    for k in range(share):
        hits = [one_hot(row * share + k == key_ref[c : c + 1, :]) for c in range(2)]
        placed = jnp.concatenate([both if j == k else zero for j in range(share)], axis=0)
        total += dot_nt(jnp.concatenate(hits, axis=1), placed)
    out_ref[...] = total.astype(BF16)


def root_sum(key, mine, theirs, rows):
    return pl.pallas_call(
        root_kernel,
        out_shape=jax.ShapeDtypeStruct((rows, LANES), BF16),
        in_specs=[VMEM, VMEM, VMEM],
        out_specs=VMEM,
        compiler_params=LIMIT,
    )(key, mine, theirs)


def last_kernel(shares_ref, load_ref, out_ref, load_out_ref):
    load_out_ref[...] = load_ref[...]
    columns, cases = out_ref.shape
    parts = cases // 2
    share = LANES // parts
    each = columns // share
    period = 2 * each
    total = jnp.zeros((16, LANES), F32)
    for s in range(shares_ref.shape[0] // 16):
        total += shares_ref[16 * s : 16 * s + 16, :].astype(F32)
    halves = total[0:period]
    for s in range(1, 16 // period):
        halves += total[s * period : (s + 1) * period]
    for k in range(share):
        lanes = halves[:, k * parts : (k + 1) * parts]
        both = jnp.concatenate([lanes[0:each], lanes[each:period]], axis=1)
        for i in range(each):
            out_ref[i * share + k : i * share + k + 1, :] = both[i : i + 1]


def last_sum(shares, load, columns):
    return pl.pallas_call(
        last_kernel,
        out_shape=(
            jax.ShapeDtypeStruct((columns, load.shape[0]), F32),
            jax.ShapeDtypeStruct(load.shape, F32),
        ),
        in_specs=[VMEM, VMEM],
        out_specs=(VMEM, VMEM),
        compiler_params=LIMIT,
    )(shares, load)


def exchange(x, axis):
    return lax.all_to_all(x, axis, split_axis=0, concat_axis=0, tiled=True)


def local(pressure, block_owner, level_one, level_one_map, level_two, level_two_map):
    members = lax.axis_size("se")
    groups = lax.axis_size("y") * lax.axis_size("core")
    core = lax.axis_index("core")
    member = lax.axis_index("se")
    cases = pressure.shape[1]
    half = level_two.shape[2]

    outgoing = pack(block_owner, pressure, members)
    incoming = exchange(outgoing, "se")

    target = level_one_map[0]
    early = bring(level_one[0])
    dest = target // half
    dofs = jnp.arange(target.shape[0], dtype=I32)
    earlier = (dest[:, None] == dest[None, :]) & (dofs[:, None] < dofs[None, :])
    slot = dest * RC + jnp.sum(earlier.astype(I32), axis=0)
    root = lax.dynamic_index_in_dim(level_two_map[0], member // 2, 0, keepdims=True)
    side = (member % 2)[None]
    partner = lax.ppermute(level_two[0], "se", [(i, i ^ 1) for i in range(members)])
    span = ROOT // groups
    roots = jnp.concatenate([root, lax.ppermute(root, "core", [(0, 1), (1, 0)])], axis=0)
    group = roots // span
    key = jnp.where(group % 2 == core, group // 2 * span + roots % span, -1)
    target, partner, key, side, early = lax.optimization_barrier((target, partner, key, side, early))

    packed = condense(incoming, early, level_one[0], slot[None, :], target[:, None], members)
    received = exchange(packed.reshape(members, RC, LANES), "se").reshape(members * RC, LANES)
    load, second = assemble(side, received, level_two[0], partner, cases)
    theirs = lax.ppermute(second, "core", [(0, 1), (1, 0)])
    columns = span // members
    share = root_sum(key, second, theirs, groups // 2 * span * (cases // 2) // LANES)
    share = exchange(share, ("y", "se"))
    root_load, level_two_load = last_sum(share, load, columns)
    return (level_two_load[None], root_load.T)


def solution(mesh):
    groups, members = mesh.devices.shape
    split = jax.sharding.Mesh(mesh.devices.reshape(groups // 2, 2, members), ("y", "core", "se"))
    grp = ("y", "core")
    every = ("y", "core", "se")
    placed = (
        P(every, None, None),
        P(every),
        P(every, None, None),
        P(every, None),
        P(grp, None, "se"),
        P(grp, None, None),
    )
    return jax.shard_map(
        local,
        mesh=split,
        in_specs=placed,
        out_specs=(P(grp, None, "se"), P(None, every)),
        check_vma=False,
    )
```

```python
import jax
import jax.numpy as jnp
from jax import lax
from jax.experimental import pallas as pl
from jax.experimental.pallas import tpu as pltpu
from jax.sharding import PartitionSpec as P

ROOT = 4096
CAPACITY = 2
RC = 16
LANES = 128
EMPTY = 64.0
BF16 = jnp.bfloat16
F32 = jnp.float32
I32 = jnp.int32
VMEM = pl.BlockSpec(memory_space=pltpu.VMEM)
SMEM = pl.BlockSpec(memory_space=pltpu.SMEM)
ANY = pl.BlockSpec(memory_space=pl.ANY)
WIDE = pltpu.CompilerParams(vmem_limit_bytes=60 * 1024 * 1024)
ROOMY = pltpu.CompilerParams(vmem_limit_bytes=16 * 1024 * 1024)
LIMIT = pltpu.CompilerParams(vmem_limit_bytes=16 * 1024 * 1024)


def iota(shape, dim):
    return lax.broadcasted_iota(I32, shape, dim)


def dot_nt(a, b):
    return lax.dot_general(a, b, (((1,), (1,)), ((), ())), preferred_element_type=F32)


def dot_tn(a, b):
    return lax.dot_general(a, b, (((0,), (0,)), ((), ())), preferred_element_type=F32)


def one_hot(hits):
    return hits.astype(F32).astype(BF16)


def pack_kernel(owner_ref, pressure_ref, out_ref, held_ref, owner_smem, count_ref, owner_sem, block_sem):
    slots = out_ref.shape[0]
    owners = pltpu.make_async_copy(owner_ref, owner_smem, owner_sem)
    blocks = pltpu.make_async_copy(pressure_ref, held_ref, block_sem)
    owners.start()
    blocks.start()
    out_ref[:, 0:16, :] = jnp.full((slots, 16, out_ref.shape[2]), EMPTY, BF16)
    for e in range(slots // CAPACITY):
        count_ref[e] = 0
    owners.wait()
    blocks.wait()
    for t in range(held_ref.shape[0]):
        owner = owner_smem[t]
        count = count_ref[owner]
        count_ref[owner] = count + 1
        out_ref[owner * CAPACITY + count] = held_ref[t]


def pack(block_owner, pressure, members):
    blocks, cases, rows = pressure.shape
    return pl.pallas_call(
        pack_kernel,
        out_shape=jax.ShapeDtypeStruct((members * CAPACITY, cases, rows), BF16),
        in_specs=[ANY, ANY],
        out_specs=VMEM,
        scratch_shapes=[
            pltpu.VMEM((blocks, cases, rows), BF16),
            pltpu.SMEM((blocks,), I32),
            pltpu.SMEM((members,), I32),
            pltpu.SemaphoreType.DMA,
            pltpu.SemaphoreType.DMA,
        ],
        compiler_params=WIDE,
    )(block_owner, pressure)


def plan_kernel(target_ref, matrix_ref, out_ref):
    out_ref[...] = target_ref[...]


def plan(target, matrix):
    return pl.pallas_call(
        plan_kernel,
        out_shape=jax.ShapeDtypeStruct(target.shape, I32),
        in_specs=[VMEM, ANY],
        out_specs=VMEM,
        compiler_params=pltpu.CompilerParams(vmem_limit_bytes=16 * 1024 * 1024),
    )(target, matrix)


def condense_kernel(
    arrived_ref, matrix_ref, slot_ref, target_ref, out_ref, incoming_ref, interior_ref, in_sem
):
    slots, cases, rows = incoming_ref.shape
    most = matrix_ref.shape[1] // rows
    arriving = pltpu.make_async_copy(arrived_ref, incoming_ref, in_sem)
    arriving.start()
    interior_ref[...] = jnp.zeros_like(interior_ref)
    arriving.wait()
    marks = incoming_ref[:, 0:16, :].astype(F32)[:, 0, 0:1]
    filled = (marks < EMPTY / 2).astype(F32)
    row, col = iota((slots, LANES), 0), iota((slots, LANES), 1)
    before = jnp.sum(jnp.where(row < col, filled, 0.0), axis=0, keepdims=True)
    here = jnp.sum(jnp.where(row == col, filled, 0.0), axis=0, keepdims=True)
    place = jnp.where(here > 0.5, before, float(most)).astype(I32) * rows
    for q in range(slots):
        at = pl.multiple_of(place[0, q], rows)
        interior_ref[0:cases, pl.ds(at, rows)] = incoming_ref[q]
    boundary = dot_nt(matrix_ref[...], interior_ref[:, 0 : most * rows])
    parts = cases // 2
    lane = iota(boundary.shape, 1)
    dest = target_ref[...] // rows
    offset = (target_ref[...] - dest * rows + 1).astype(F32)
    own = jnp.where(lane == cases + parts, offset, jnp.where(lane < cases, boundary, 0.0))
    lower = pltpu.roll(boundary, cases, 1)
    upper = pltpu.roll(boundary, parts, 1)
    other = jnp.where(dest % 2 == 1, lower, upper)
    other = jnp.where((lane >= cases) & (lane < cases + parts), other, 0.0)
    other = jnp.where(lane == cases + parts + 1, offset, other)
    slot = slot_ref[...]
    choose = one_hot(slot == iota((out_ref.shape[0], slot.shape[1]), 0))
    both = jnp.concatenate([own, other], axis=1).astype(BF16)
    chosen = jnp.dot(choose, both, preferred_element_type=F32)
    blocks = chosen[:, LANES : 2 * LANES].reshape(-1, 2, RC, LANES)
    swapped = jnp.concatenate([blocks[:, 1:2], blocks[:, 0:1]], axis=1)
    sent = chosen[:, 0:LANES] + swapped.reshape(-1, LANES)
    out_ref[...] = sent.astype(BF16)


def condense(incoming, matrix, slot, target, members):
    depth = matrix.shape[1]
    rows = incoming.shape[2]
    return pl.pallas_call(
        condense_kernel,
        out_shape=jax.ShapeDtypeStruct((members * RC, LANES), BF16),
        in_specs=[ANY, VMEM, VMEM, VMEM],
        out_specs=VMEM,
        scratch_shapes=[
            pltpu.VMEM(incoming.shape, BF16),
            pltpu.VMEM((LANES, depth + rows), BF16),
            pltpu.SemaphoreType.DMA,
        ],
        compiler_params=ROOMY,
    )(incoming, matrix, slot, target)


def assemble_kernel(side_ref, rows_ref, matrix_ref, other_ref, load_ref, out_ref):
    cases = load_ref.shape[0]
    parts = cases // 2
    rows = rows_ref[...]
    offsets = rows.astype(F32)[:, cases + parts : cases + parts + 2]
    want = (iota(rows.shape, 1) + 1).astype(F32)
    hits = jnp.concatenate([one_hot(offsets[:, 0:1] == want), one_hot(offsets[:, 1:2] == want)], axis=1)
    loads = dot_tn(rows, hits)
    load = loads[0:cases, 0:LANES]
    other = loads[cases : cases + parts, LANES : 2 * LANES]
    load_ref[...] = load
    second = dot_nt(load.astype(BF16), matrix_ref[...])
    second = jnp.where(side_ref[0] == 0, second[0:parts], second[parts:cases])
    out_ref[...] = (second + dot_nt(other.astype(BF16), other_ref[...])).astype(BF16)


def assemble(side, rows, matrix, other, cases):
    half = matrix.shape[1]
    return pl.pallas_call(
        assemble_kernel,
        out_shape=(
            jax.ShapeDtypeStruct((cases, half), F32),
            jax.ShapeDtypeStruct((cases // 2, LANES), BF16),
        ),
        in_specs=[SMEM, VMEM, VMEM, VMEM],
        out_specs=(VMEM, VMEM),
        compiler_params=LIMIT,
    )(side, rows, matrix, other)


def root_kernel(key_ref, mine_ref, theirs_ref, out_ref):
    rows = out_ref.shape[0]
    parts = mine_ref.shape[0]
    share = LANES // parts
    row = iota((rows, LANES), 0)
    both = jnp.concatenate([mine_ref[...], theirs_ref[...]], axis=1)
    zero = jnp.zeros_like(both)
    total = jnp.zeros(out_ref.shape, F32)
    for k in range(share):
        hits = [one_hot(row * share + k == key_ref[c : c + 1, :]) for c in range(2)]
        placed = jnp.concatenate([both if j == k else zero for j in range(share)], axis=0)
        total += dot_nt(jnp.concatenate(hits, axis=1), placed)
    out_ref[...] = total.astype(BF16)


def root_sum(key, mine, theirs, rows):
    return pl.pallas_call(
        root_kernel,
        out_shape=jax.ShapeDtypeStruct((rows, LANES), BF16),
        in_specs=[VMEM, VMEM, VMEM],
        out_specs=VMEM,
        compiler_params=LIMIT,
    )(key, mine, theirs)


def last_kernel(shares_ref, load_ref, out_ref, load_out_ref):
    load_out_ref[...] = load_ref[...]
    columns, cases = out_ref.shape
    parts = cases // 2
    share = LANES // parts
    each = columns // share
    period = 2 * each
    total = jnp.zeros((16, LANES), F32)
    for s in range(shares_ref.shape[0] // 16):
        total += shares_ref[16 * s : 16 * s + 16, :].astype(F32)
    halves = total[0:period]
    for s in range(1, 16 // period):
        halves += total[s * period : (s + 1) * period]
    for k in range(share):
        lanes = halves[:, k * parts : (k + 1) * parts]
        both = jnp.concatenate([lanes[0:each], lanes[each:period]], axis=1)
        for i in range(each):
            out_ref[i * share + k : i * share + k + 1, :] = both[i : i + 1]


def last_sum(shares, load, columns):
    return pl.pallas_call(
        last_kernel,
        out_shape=(
            jax.ShapeDtypeStruct((columns, load.shape[0]), F32),
            jax.ShapeDtypeStruct(load.shape, F32),
        ),
        in_specs=[VMEM, VMEM],
        out_specs=(VMEM, VMEM),
        compiler_params=LIMIT,
    )(shares, load)


def exchange(x, axis):
    return lax.all_to_all(x, axis, split_axis=0, concat_axis=0, tiled=True)


def local(pressure, block_owner, level_one, level_one_map, level_two, level_two_map):
    members = lax.axis_size("se")
    groups = lax.axis_size("y") * lax.axis_size("core")
    core = lax.axis_index("core")
    member = lax.axis_index("se")
    cases = pressure.shape[1]
    half = level_two.shape[2]

    outgoing = pack(block_owner, pressure, members)
    incoming = exchange(outgoing, "se")

    target = plan(level_one_map, level_one[0])[0]
    dest = target // half
    dofs = jnp.arange(target.shape[0], dtype=I32)
    earlier = (dest[:, None] == dest[None, :]) & (dofs[:, None] < dofs[None, :])
    slot = dest * RC + jnp.sum(earlier.astype(I32), axis=0)
    root = lax.dynamic_index_in_dim(level_two_map[0], member // 2, 0, keepdims=True)
    side = (member % 2)[None]
    partner = lax.ppermute(level_two[0], "se", [(i, i ^ 1) for i in range(members)])
    span = ROOT // groups
    roots = jnp.concatenate([root, lax.ppermute(root, "core", [(0, 1), (1, 0)])], axis=0)
    group = roots // span
    key = jnp.where(group % 2 == core, group // 2 * span + roots % span, -1)
    target, partner, key, side = lax.optimization_barrier((target, partner, key, side))

    packed = condense(incoming, level_one[0], slot[None, :], target[:, None], members)
    received = exchange(packed.reshape(members, RC, LANES), "se").reshape(members * RC, LANES)
    load, second = assemble(side, received, level_two[0], partner, cases)
    theirs = lax.ppermute(second, "core", [(0, 1), (1, 0)])
    columns = span // members
    share = root_sum(key, second, theirs, groups // 2 * span * (cases // 2) // LANES)
    share = exchange(share, ("y", "se"))
    root_load, level_two_load = last_sum(share, load, columns)
    return (level_two_load[None], root_load.T)


def solution(mesh):
    groups, members = mesh.devices.shape
    split = jax.sharding.Mesh(mesh.devices.reshape(groups // 2, 2, members), ("y", "core", "se"))
    grp = ("y", "core")
    every = ("y", "core", "se")
    placed = (
        P(every, None, None),
        P(every),
        P(every, None, None),
        P(every, None),
        P(grp, None, "se"),
        P(grp, None, None),
    )
    return jax.shard_map(
        local,
        mesh=split,
        in_specs=placed,
        out_specs=(P(grp, None, "se"), P(None, every)),
        check_vma=False,
    )
```

```python
import jax
import jax.numpy as jnp
from jax import lax
from jax.experimental import pallas as pl
from jax.experimental.pallas import tpu as pltpu
from jax.sharding import PartitionSpec as P

ROOT = 4096
CAPACITY = 2
RC = 16
LANES = 128
EARLY = 3072
EMPTY = 64.0
BF16 = jnp.bfloat16
F32 = jnp.float32
I32 = jnp.int32
VMEM = pl.BlockSpec(memory_space=pltpu.VMEM)
SMEM = pl.BlockSpec(memory_space=pltpu.SMEM)
ANY = pl.BlockSpec(memory_space=pl.ANY)
WIDE = pltpu.CompilerParams(vmem_limit_bytes=62 * 1024 * 1024)
ROOMY = pltpu.CompilerParams(vmem_limit_bytes=50 * 1024 * 1024)
LIMIT = pltpu.CompilerParams(vmem_limit_bytes=16 * 1024 * 1024)


def iota(shape, dim):
    return lax.broadcasted_iota(I32, shape, dim)


def dot_nt(a, b):
    return lax.dot_general(a, b, (((1,), (1,)), ((), ())), preferred_element_type=F32)


def dot_tn(a, b):
    return lax.dot_general(a, b, (((0,), (0,)), ((), ())), preferred_element_type=F32)


def one_hot(hits):
    return hits.astype(F32).astype(BF16)


def pack_kernel(owner_ref, pressure_ref, out_ref, held_ref, owner_smem, count_ref, owner_sem, block_sem):
    slots = out_ref.shape[0]
    owners = pltpu.make_async_copy(owner_ref, owner_smem, owner_sem)
    half = held_ref.shape[0] // 2
    halves = []
    for h in range(2):
        part = slice(h * half, held_ref.shape[0] if h else half)
        halves.append(pltpu.make_async_copy(pressure_ref.at[part], held_ref.at[part], block_sem.at[h]))
    owners.start()
    for copy in halves:
        copy.start()
    out_ref[:, 0:16, :] = jnp.full((slots, 16, out_ref.shape[2]), EMPTY, BF16)
    for e in range(slots // CAPACITY):
        count_ref[e] = 0
    owners.wait()
    for t in range(held_ref.shape[0]):
        if t == 0 or t == half:
            halves[t // half].wait()
        owner = owner_smem[t]
        count = count_ref[owner]
        count_ref[owner] = count + 1
        out_ref[owner * CAPACITY + count] = held_ref[t]


def pack(block_owner, pressure, members):
    blocks, cases, rows = pressure.shape
    return pl.pallas_call(
        pack_kernel,
        out_shape=jax.ShapeDtypeStruct((members * CAPACITY, cases, rows), BF16),
        in_specs=[ANY, ANY],
        out_specs=VMEM,
        scratch_shapes=[
            pltpu.VMEM((blocks, cases, rows), BF16),
            pltpu.SMEM((blocks,), I32),
            pltpu.SMEM((members,), I32),
            pltpu.SemaphoreType.DMA,
            pltpu.SemaphoreType.DMA((2,)),
        ],
        compiler_params=WIDE,
    )(block_owner, pressure)


def bring_kernel(level_ref, out_ref, sem):
    copy = pltpu.make_async_copy(level_ref.at[:, 0 : out_ref.shape[1]], out_ref, sem)
    copy.start()
    copy.wait()


def bring(matrix):
    return pl.pallas_call(
        bring_kernel,
        out_shape=jax.ShapeDtypeStruct((matrix.shape[0], EARLY), BF16),
        in_specs=[ANY],
        out_specs=VMEM,
        scratch_shapes=[pltpu.SemaphoreType.DMA],
        compiler_params=pltpu.CompilerParams(vmem_limit_bytes=48 * 1024 * 1024),
    )(matrix)


def condense_kernel(
    incoming_ref, early_ref, level_ref, slot_ref, target_ref, out_ref, late_ref, interior_ref, level_sem
):
    slots, cases, rows = incoming_ref.shape
    depth = level_ref.shape[1]
    most = depth // rows
    late = pltpu.make_async_copy(level_ref.at[:, EARLY:depth], late_ref, level_sem)
    late.start()
    interior_ref[...] = jnp.zeros_like(interior_ref)
    marks = incoming_ref[:, 0:16, :].astype(F32)[:, 0, 0:1]
    filled = (marks < EMPTY / 2).astype(F32)
    row, col = iota((slots, LANES), 0), iota((slots, LANES), 1)
    before = jnp.sum(jnp.where(row < col, filled, 0.0), axis=0, keepdims=True)
    here = jnp.sum(jnp.where(row == col, filled, 0.0), axis=0, keepdims=True)
    place = jnp.where(here > 0.5, before, float(most)).astype(I32) * rows
    for q in range(slots):
        at = pl.multiple_of(place[0, q], rows)
        interior_ref[0:cases, pl.ds(at, rows)] = incoming_ref[q]
    boundary = dot_nt(early_ref[...], interior_ref[:, 0:EARLY])
    late.wait()
    boundary += dot_nt(late_ref[...], interior_ref[:, EARLY:depth])
    parts = cases // 2
    lane = iota(boundary.shape, 1)
    dest = target_ref[...] // rows
    offset = (target_ref[...] - dest * rows + 1).astype(F32)
    own = jnp.where(lane == cases + parts, offset, jnp.where(lane < cases, boundary, 0.0))
    lower = pltpu.roll(boundary, cases, 1)
    upper = pltpu.roll(boundary, parts, 1)
    other = jnp.where(dest % 2 == 1, lower, upper)
    other = jnp.where((lane >= cases) & (lane < cases + parts), other, 0.0)
    other = jnp.where(lane == cases + parts + 1, offset, other)
    slot = slot_ref[...]
    choose = one_hot(slot == iota((out_ref.shape[0], slot.shape[1]), 0))
    both = jnp.concatenate([own, other], axis=1).astype(BF16)
    chosen = jnp.dot(choose, both, preferred_element_type=F32)
    blocks = chosen[:, LANES : 2 * LANES].reshape(-1, 2, RC, LANES)
    swapped = jnp.concatenate([blocks[:, 1:2], blocks[:, 0:1]], axis=1)
    sent = chosen[:, 0:LANES] + swapped.reshape(-1, LANES)
    out_ref[...] = sent.astype(BF16)


def condense(incoming, early, matrix, slot, target, members):
    depth = matrix.shape[1]
    rows = incoming.shape[2]
    return pl.pallas_call(
        condense_kernel,
        out_shape=jax.ShapeDtypeStruct((members * RC, LANES), BF16),
        in_specs=[VMEM, VMEM, ANY, VMEM, VMEM],
        out_specs=VMEM,
        scratch_shapes=[
            pltpu.VMEM((matrix.shape[0], depth - EARLY), BF16),
            pltpu.VMEM((LANES, depth + rows), BF16),
            pltpu.SemaphoreType.DMA,
        ],
        compiler_params=ROOMY,
    )(incoming, early, matrix, slot, target)


def assemble_kernel(side_ref, rows_ref, matrix_ref, other_ref, load_ref, out_ref):
    cases = load_ref.shape[0]
    parts = cases // 2
    rows = rows_ref[...]
    offsets = rows.astype(F32)[:, cases + parts : cases + parts + 2]
    want = (iota(rows.shape, 1) + 1).astype(F32)
    hits = jnp.concatenate([one_hot(offsets[:, 0:1] == want), one_hot(offsets[:, 1:2] == want)], axis=1)
    loads = dot_tn(rows, hits)
    load = loads[0:cases, 0:LANES]
    other = loads[cases : cases + parts, LANES : 2 * LANES]
    load_ref[...] = load
    second = dot_nt(load.astype(BF16), matrix_ref[...])
    second = jnp.where(side_ref[0] == 0, second[0:parts], second[parts:cases])
    out_ref[...] = (second + dot_nt(other.astype(BF16), other_ref[...])).astype(BF16)


def assemble(side, rows, matrix, other, cases):
    half = matrix.shape[1]
    return pl.pallas_call(
        assemble_kernel,
        out_shape=(
            jax.ShapeDtypeStruct((cases, half), F32),
            jax.ShapeDtypeStruct((cases // 2, LANES), BF16),
        ),
        in_specs=[SMEM, VMEM, VMEM, VMEM],
        out_specs=(VMEM, VMEM),
        compiler_params=LIMIT,
    )(side, rows, matrix, other)


def root_kernel(key_ref, mine_ref, theirs_ref, out_ref):
    rows = out_ref.shape[0]
    parts = mine_ref.shape[0]
    share = LANES // parts
    row = iota((rows, LANES), 0)
    both = jnp.concatenate([mine_ref[...], theirs_ref[...]], axis=1)
    zero = jnp.zeros_like(both)
    total = jnp.zeros(out_ref.shape, F32)
    for k in range(share):
        hits = [one_hot(row * share + k == key_ref[c : c + 1, :]) for c in range(2)]
        placed = jnp.concatenate([both if j == k else zero for j in range(share)], axis=0)
        total += dot_nt(jnp.concatenate(hits, axis=1), placed)
    out_ref[...] = total.astype(BF16)


def root_sum(key, mine, theirs, rows):
    return pl.pallas_call(
        root_kernel,
        out_shape=jax.ShapeDtypeStruct((rows, LANES), BF16),
        in_specs=[VMEM, VMEM, VMEM],
        out_specs=VMEM,
        compiler_params=LIMIT,
    )(key, mine, theirs)


def last_kernel(shares_ref, load_ref, out_ref, load_out_ref):
    load_out_ref[...] = load_ref[...]
    columns, cases = out_ref.shape
    parts = cases // 2
    share = LANES // parts
    each = columns // share
    period = 2 * each
    total = jnp.zeros((16, LANES), F32)
    for s in range(shares_ref.shape[0] // 16):
        total += shares_ref[16 * s : 16 * s + 16, :].astype(F32)
    halves = total[0:period]
    for s in range(1, 16 // period):
        halves += total[s * period : (s + 1) * period]
    for k in range(share):
        lanes = halves[:, k * parts : (k + 1) * parts]
        both = jnp.concatenate([lanes[0:each], lanes[each:period]], axis=1)
        for i in range(each):
            out_ref[i * share + k : i * share + k + 1, :] = both[i : i + 1]


def last_sum(shares, load, columns):
    return pl.pallas_call(
        last_kernel,
        out_shape=(
            jax.ShapeDtypeStruct((columns, load.shape[0]), F32),
            jax.ShapeDtypeStruct(load.shape, F32),
        ),
        in_specs=[VMEM, VMEM],
        out_specs=(VMEM, VMEM),
        compiler_params=LIMIT,
    )(shares, load)


def exchange(x, axis):
    return lax.all_to_all(x, axis, split_axis=0, concat_axis=0, tiled=True)


def local(pressure, block_owner, level_one, level_one_map, level_two, level_two_map):
    members = lax.axis_size("se")
    groups = lax.axis_size("y") * lax.axis_size("core")
    core = lax.axis_index("core")
    member = lax.axis_index("se")
    cases = pressure.shape[1]
    half = level_two.shape[2]

    outgoing = pack(block_owner, pressure, members)
    incoming = exchange(outgoing, "se")

    target = level_one_map[0]
    early = bring(level_one[0])
    dest = target // half
    dofs = jnp.arange(target.shape[0], dtype=I32)
    earlier = (dest[:, None] == dest[None, :]) & (dofs[:, None] < dofs[None, :])
    slot = dest * RC + jnp.sum(earlier.astype(I32), axis=0)
    root = lax.dynamic_index_in_dim(level_two_map[0], member // 2, 0, keepdims=True)
    side = (member % 2)[None]
    partner = lax.ppermute(level_two[0], "se", [(i, i ^ 1) for i in range(members)])
    span = ROOT // groups
    roots = jnp.concatenate([root, lax.ppermute(root, "core", [(0, 1), (1, 0)])], axis=0)
    group = roots // span
    key = jnp.where(group % 2 == core, group // 2 * span + roots % span, -1)
    target, partner, key, side, early = lax.optimization_barrier((target, partner, key, side, early))

    packed = condense(incoming, early, level_one[0], slot[None, :], target[:, None], members)
    received = exchange(packed.reshape(members, RC, LANES), "se").reshape(members * RC, LANES)
    load, second = assemble(side, received, level_two[0], partner, cases)
    theirs = lax.ppermute(second, "core", [(0, 1), (1, 0)])
    columns = span // members
    share = root_sum(key, second, theirs, groups // 2 * span * (cases // 2) // LANES)
    share = exchange(share, ("y", "se"))
    root_load, level_two_load = last_sum(share, load, columns)
    return (level_two_load[None], root_load.T)


def solution(mesh):
    groups, members = mesh.devices.shape
    split = jax.sharding.Mesh(mesh.devices.reshape(groups // 2, 2, members), ("y", "core", "se"))
    grp = ("y", "core")
    every = ("y", "core", "se")
    placed = (
        P(every, None, None),
        P(every),
        P(every, None, None),
        P(every, None),
        P(grp, None, "se"),
        P(grp, None, None),
    )
    return jax.shard_map(
        local,
        mesh=split,
        in_specs=placed,
        out_specs=(P(grp, None, "se"), P(None, every)),
        check_vma=False,
    )
```
